512 devices in a mesh: row: 8 (over y), col: 8 (over x, z_hi), tp: 8 (over z_lo, core).
Axes of the slice: x: 4, y: 8, z: 8 (z_hi: 2, z_lo: 4; z = z_hi * 4 + z_lo), core: 2. Of those that a mesh axis runs over, the one named last changes fastest.
Arguments:
- act_one: bfloat16 [8, 8, 256, 8192], P('row', 'col', None, 'tp'), may hold values from -6 to 6
- residual: bfloat16 [8, 8, 256, 2048], P('row', 'col', None, 'tp'), may hold values from -6 to 6
- upstream: bfloat16 [8, 8, 256, 8192], P('row', 'col', None, 'tp'), may hold values from -6 to 6
- stream_grad: bfloat16 [8, 8, 256, 256], P('row', 'col'), may hold values from -6 to 6
- token_ids: int32 [8, 8, 256], P('row', 'col'), may hold values from 0 to 31999, as said below
- shard_counts: int32 [8, 8], P('row', 'col'), may hold values from 4096 to 106807
- out_one: bfloat16 [8, 8192, 2048], P('col', 'tp', 'row'), may hold values from -6 to 6
- in_two: bfloat16 [8, 8192, 2048], P('row', 'tp', 'col'), may hold values from -6 to 6
- out_one_moment: float32 [8, 8192, 256], P('col', 'tp', 'row'), may hold values from -3 to 3
- in_two_moment: float32 [8, 8192, 256], P('row', 'tp', 'col'), may hold values from -3 to 3
Outputs:
- out_one_new: float32 [8, 8192, 256], P('col', 'tp', 'row')
- out_one_moment_new: float32 [8, 8192, 256], P('col', 'tp', 'row')
- in_two_new: float32 [8, 8192, 256], P('row', 'tp', 'col')
- in_two_moment_new: float32 [8, 8192, 256], P('row', 'tp', 'col')
The draws below stay inside these ranges and needn't reach their ends.
Inputs may be any that keep to these rules, and one draw needn't show every extreme that they name: `token_ids`: id 0 marks padding and appears only at the end of a path's tokens.
All inputs are finite; a program needn't handle non-finite values.
Results may differ from the reference program's by a relative error of at most 0.017.
Values may be sent and summed in bfloat16 or wider, within the bound.
A program may use at most 64 MiB of HBM per device.

```python
import jax
import jax.numpy as jnp
from jax import lax

D = 2048
H = 8192
VOCAB = 32000
TOK = 256
COLS = 256
GR = 8
GC = 8
N_ROW = 8
N_COL = 8
N_TP = 8


def draw_token_ids(key, part):
    first_key, second_key = jax.random.split(jax.random.fold_in(key, 11))
    raw_ids = jax.random.randint(first_key, (GR, GC, TOK), 1, VOCAB)
    pad_len = jax.random.randint(second_key, (GR, GC, 1), 0, TOK // 2 + 1)
    position = jnp.arange(TOK)[None, None, :]
    return jnp.where(position < TOK - pad_len, raw_ids, 0).astype(jnp.int32)


def draw_shard_counts(key, part):
    base_draw = jax.random.randint(jax.random.fold_in(key, 23), (GR, GC), 64, 128)
    row_steps = jnp.arange(GR, dtype=jnp.int32)[:, None]
    col_steps = jnp.arange(GC, dtype=jnp.int32)[None, :]
    first_cell = (row_steps == 0) & (col_steps == 0)
    last_cell = (row_steps == GR - 1) & (col_steps == GC - 1)
    base_draw = jnp.where(first_cell, 64, base_draw)
    base_draw = jnp.where(last_cell, 127, base_draw)
    return (base_draw * (GR + 3 * row_steps) * (GC + 3 * col_steps)).astype(jnp.int32)


def steps_of(own_key, dims, cuts, least, high):
    level = 1.0
    for dim, blocks in cuts:
        draws = jax.random.uniform(jax.random.fold_in(jax.random.fold_in(own_key, 6), dim), (blocks,), jnp.float32, least / len(cuts), high / len(cuts))
        level = level * jnp.repeat(jnp.exp(draws), dims[dim] // blocks).reshape((-1,) + (1,) * (len(dims) - 1 - dim))
    return level


def noise(key, extent, spread, limit, cuts=(), kind=jnp.bfloat16):
    array = jax.random.normal(key, extent, jnp.float32) * spread
    if len(cuts) > 0:
        array = steps_of(key, extent, cuts, -0.22, 0.18) * array
    return jnp.clip(array, min=-limit, max=limit).astype(kind)


def setup_inputs(seed: int = 0) -> dict:
    key_of = jax.random.split(jax.random.key(seed), 11)
    act_one = noise(key_of[0], (GR, GC, TOK, H), 1.0, 6.0, ((0, 8), (1, 8), (3, 8)))
    residual = noise(key_of[1], (GR, GC, TOK, D), 1.0, 6.0, ((0, 8), (1, 8), (3, 8)))
    upstream = noise(key_of[2], (GR, GC, TOK, H), 1.0, 6.0, ((0, 8), (1, 8), (3, 8)))
    stream_grad = noise(key_of[3], (GR, GC, TOK, COLS), 1.0, 6.0, ((0, 8), (1, 8)))
    token_ids = draw_token_ids(jax.random.fold_in(key_of[10], 71), 0)
    shard_counts = draw_shard_counts(jax.random.fold_in(key_of[10], 71), 0)
    out_one = noise(key_of[6], (GC, H, D), 1.0, 6.0, ((0, 8), (1, 8), (2, 8)))
    in_two = noise(key_of[7], (GR, H, D), 1.0, 6.0, ((0, 8), (1, 8), (2, 8)))
    out_one_moment = noise(key_of[8], (GC, H, COLS), 0.5, 3.0, ((0, 8), (1, 8), (2, 8)), jnp.float32)
    in_two_moment = noise(key_of[9], (GR, H, COLS), 0.5, 3.0, ((0, 8), (1, 8), (2, 8)), jnp.float32)
    return dict(act_one=act_one, residual=residual, upstream=upstream, stream_grad=stream_grad, token_ids=token_ids, shard_counts=shard_counts, out_one=out_one, in_two=in_two, out_one_moment=out_one_moment, in_two_moment=in_two_moment)


inner_rate = 4.0
outer_rate = 0.7
momentum_decay = 0.9


def pick_columns(matrix, groups):
    rows = matrix.shape[0]
    return matrix.reshape(rows, groups, D // groups)[:, :, :COLS // groups].reshape(rows, COLS)


def hidden_groups(left, right, scale):
    count = left.shape[0]
    group = H // N_TP
    left_groups = left.reshape(count, N_TP, group).astype(jnp.float32)
    right_groups = right.reshape(N_TP, group, right.shape[1]).astype(jnp.float32)
    partial_value = jnp.einsum("tjh,jhd->jtd", left_groups, right_groups) * scale
    return jnp.sum(lax.optimization_barrier(partial_value.astype(jnp.bfloat16)).astype(jnp.float32), axis=0)


def path_grads(act_rows, resid_rows, up_rows, stream_rows, path_ids, first_weight, second_weight):
    scale_model = 1.0 / (D ** 0.5)
    scale_hidden = 1.0 / (H ** 0.5)
    keep = (path_ids != 0)[:, None]
    masked_up = jnp.where(keep, up_rows, jnp.zeros_like(up_rows))
    masked_stream = jnp.where(keep, stream_rows, jnp.zeros_like(stream_rows))
    summed = hidden_groups(act_rows, first_weight, scale_hidden)
    stream_rows_new = (resid_rows.astype(jnp.float32) + summed).astype(jnp.bfloat16)
    pre_second = jnp.dot(stream_rows_new, second_weight.T, preferred_element_type=jnp.float32) * scale_model
    squash = jax.nn.sigmoid(pre_second)
    slope = (masked_up.astype(jnp.float32) * squash * (1.0 + pre_second * (1.0 - squash))).astype(jnp.bfloat16)
    grad_two = jnp.dot(slope.T, pick_columns(stream_rows_new, N_COL), preferred_element_type=jnp.float32) * scale_model
    carried = hidden_groups(slope, pick_columns(second_weight, N_ROW), scale_model)
    stream_back = (masked_stream.astype(jnp.float32) + carried).astype(jnp.bfloat16)
    grad_one = jnp.dot(act_rows.T, stream_back, preferred_element_type=jnp.float32) * scale_hidden
    return grad_one, grad_two


def rounded_term(weight, grad):
    return lax.optimization_barrier((weight * inner_rate * grad).astype(jnp.bfloat16)).astype(jnp.float32)


def outer_step(picked, moment, summed, total):
    delta = summed / total[:, None, None]
    moment_new = momentum_decay * moment + delta
    fresh = picked.astype(jnp.float32) - outer_rate * (delta + momentum_decay * moment_new)
    return fresh, moment_new


def reference(act_one, residual, upstream, stream_grad, token_ids, shard_counts, out_one, in_two, out_one_moment, in_two_moment):
    counts = shard_counts.astype(jnp.float32)
    start = (jnp.zeros((GC, H, COLS), jnp.float32), jnp.zeros((GR, H, COLS), jnp.float32))

    def visit(carried, path_index):
        sum_one, sum_two = carried
        row_at = path_index // GC
        col_at = path_index % GC
        grads = path_grads(act_one[row_at, col_at], residual[row_at, col_at], upstream[row_at, col_at], stream_grad[row_at, col_at], token_ids[row_at, col_at], out_one[col_at], in_two[row_at])
        weight = counts[row_at, col_at]
        sum_one = sum_one.at[col_at].add(rounded_term(weight, grads[0]))
        sum_two = sum_two.at[row_at].add(rounded_term(weight, grads[1]))
        return (sum_one, sum_two), None

    sums, _ = lax.scan(visit, start, jnp.arange(GR * GC, dtype=jnp.int32))
    total_one = jnp.sum(counts, axis=0)
    total_two = jnp.sum(counts, axis=1)
    picked_one = jax.vmap(lambda matrix: pick_columns(matrix, N_ROW))(out_one)
    picked_two = jax.vmap(lambda matrix: pick_columns(matrix, N_COL))(in_two)
    out_one_new, out_one_moment_new = outer_step(picked_one, out_one_moment, sums[0], total_one)
    in_two_new, in_two_moment_new = outer_step(picked_two, in_two_moment, sums[1], total_two)
    return out_one_new, out_one_moment_new, in_two_new, in_two_moment_new
```

```python
import math

import jax
import jax.numpy as jnp
from jax import lax
from jax.experimental import pallas as pl
from jax.experimental.pallas import tpu as pltpu
from jax.sharding import PartitionSpec as P

D = 2048
H = 8192
TOK = 256
HID = 1024
BLK = 256
SEL = 32
INNER = 4.0
OUTER = 0.7
DECAY = 0.9
MESH = pl.DeviceIdType.MESH
BF = jnp.bfloat16
F32 = jnp.float32

SCALE_MODEL = 1.0 / math.sqrt(D)
SCALE_HIDDEN = 1.0 / math.sqrt(H)
NT = (((1,), (1,)), ((), ()))
OFFSETS = (0, 7, 1, 6, 2, 5, 3, 4)


def kernel(
    act_h, res_h, up_h, st_h, ids_h, cnt_v, w1_h, w2_h, m1_h, m2_h,
    o1, n1, o2, n2,
    act, res, up, st, ids, w1g, w2g, m1, m2,
    part, cin, zb, zin, y, relay, pre2, slope, selw, sely, stt, pc1, pc2,
    q, qin, dy, t1, t1in, t2, t2x, t2z, t2zin, wown, wrow, wcol,
    loc, w1s, w1r, w2s, w2r, zs, zr,
    crs, crr, zrs, zrr, ags, agr, cgs, cgr,
    qs, qr, ds_, dr_, rs_, rr_, xs, xr, as_, ar_, nrs, nrr, ncs, ncr,
):
    r = lax.axis_index("row")
    c = lax.axis_index("col")
    t = lax.axis_index("tp")
    x = lax.div(c, 2)
    zh = lax.rem(c, 2)
    zl = lax.div(t, 2)
    core = lax.rem(t, 2)
    z = zh * 4 + zl
    other = (r, c, zl * 2 + 1 - core)

    def row_dev(d):
        return (lax.rem(r + d, 8), c, t)

    def tp_dev(d):
        return (r, c, lax.rem(t + d, 8))

    def x_dev(d):
        return (r, lax.rem(x + d, 4) * 2 + zh, t)

    def z_dev(d):
        to = lax.rem(z + d, 8)
        return (r, x * 2 + lax.div(to, 4), lax.rem(to, 4) * 2 + core)

    def zl_dev(d):
        return (r, c, lax.rem(zl + d, 4) * 2 + core)

    def col_dev(d):
        return (r, lax.rem(c + d, 8), t)

    antipode = (r, x * 2 + 1 - zh, t)
    pending = []

    def send(src, dst, s_sem, r_sem, device):
        copy = pltpu.make_async_remote_copy(
            src_ref=src, dst_ref=dst, send_sem=s_sem, recv_sem=r_sem,
            device_id=device, device_id_type=MESH,
        )
        copy.start()
        pending.append(copy)

    def arrive(dst, s_sem, r_sem):
        pltpu.make_async_remote_copy(
            src_ref=dst, dst_ref=dst, send_sem=s_sem, recv_sem=r_sem,
            device_id=other, device_id_type=MESH,
        ).wait_recv()

    local = [
        pltpu.make_async_copy(a, b, loc.at[k])
        for k, (a, b) in enumerate(
            (
                (w1_h, w1g.at[r]), (w2_h, w2g.at[c]), (act_h, act), (res_h, res),
                (up_h, up), (st_h, st), (ids_h, ids), (m1_h, m1), (m2_h, m2),
            )
        )
    ]
    for copy in local:
        copy.start()

    barrier = pltpu.get_barrier_semaphore()
    partners = (
        [row_dev(d) for d in range(1, 8)]
        + [col_dev(d) for d in range(1, 8)]
        + [tp_dev(d) for d in range(1, 8)]
        + [z_dev(2), z_dev(6)]
    )
    for device in partners:
        pl.semaphore_signal(barrier, inc=1, device_id=device, device_id_type=MESH)
    weight = cnt_v[...].astype(F32)
    wown[...] = jnp.broadcast_to(weight, (8, 128))
    pl.semaphore_wait(barrier, len(partners))

    def w1_chunk(n, half):
        return w1g.at[n, pl.ds(512 * half, 512)]

    def w1_send(way, step, j):
        n = lax.rem(r + (8 - step if way == 0 else step), 8)
        half = j if way == 0 else 1 - j
        ref = w1_chunk(n, half)
        send(ref, ref, w1s.at[way, step, j], w1r.at[way, step, j], row_dev(1 if way == 0 else 7))

    def w1_wait(way, step, j):
        n = lax.rem(r + (7 - step if way == 0 else step + 1), 8)
        half = j if way == 0 else 1 - j
        arrive(w1_chunk(n, half), w1s.at[way, step, j], w1r.at[way, step, j])

    def w2_chunk(at, phase, half):
        plane = zh if phase == 0 else 1 - zh
        return w2g.at[lax.rem(at, 4) * 2 + plane, pl.ds(512 * half, 512)]

    def w2_send(phase, way, j):
        half = j % 2 if way == 0 else 1 - j % 2
        back = 0 if j < 2 else 1
        at = x + (4 - back if way == 0 else back)
        ref = w2_chunk(at, phase, half)
        send(ref, ref, w2s.at[phase, way, j], w2r.at[phase, way, j], x_dev(1 if way == 0 else 3))

    def w2_wait(phase, way, j):
        half = j % 2 if way == 0 else 1 - j % 2
        back = 1 if j < 2 else 2
        at = x + (4 - back if way == 0 else back)
        arrive(w2_chunk(at, phase, half), w2s.at[phase, way, j], w2r.at[phase, way, j])

    def z_first(way):
        send(
            w2g.at[c, pl.ds(512 * way, 512)], relay.at[way],
            zs.at[way, 0], zr.at[way, 0], z_dev(2 if way == 0 else 6),
        )

    def z_second(way):
        arrive(relay.at[way], zs.at[way, 0], zr.at[way, 0])
        hop = 2 if way == 0 else 6
        far = lax.div(lax.rem(z + hop, 8), 4)
        send(
            relay.at[way], w2g.at[x * 2 + 1 - far, pl.ds(512 * way, 512)],
            zs.at[way, 1], zr.at[way, 1], z_dev(hop),
        )

    def z_wait(way):
        arrive(w2g.at[x * 2 + 1 - zh, pl.ds(512 * way, 512)], zs.at[way, 1], zr.at[way, 1])

    local[0].wait()
    for j in range(2):
        for way in range(2):
            w1_send(way, 0, j)
    local[1].wait()
    for j in range(2):
        for way in range(2):
            w2_send(0, way, j)
    for way in range(2):
        z_first(way)
    for d in range(1, 8):
        send(wown, wrow.at[d - 1], nrs.at[d - 1], nrr.at[d - 1], row_dev(d))
        send(wown, wcol.at[d - 1], ncs.at[d - 1], ncr.at[d - 1], col_dev(d))
    for copy in local[2:]:
        copy.wait()

    def block(i):
        return lax.rem(r + OFFSETS[i], 8)

    def stage0(i):
        n = block(i)
        acc = jnp.dot(act[...], w1g[n], preferred_element_type=F32) * SCALE_HIDDEN
        mine = jnp.where(n == t, 1.0, 0.0).astype(F32)
        acc = acc + res[...].astype(F32) * mine
        part[i] = acc.astype(BF).reshape(2, 128, BLK)
        send(part.at[i, 1 - core], cin.at[i], crs.at[i], crr.at[i], other)

    def stage1(i):
        arrive(cin.at[i], crs.at[i], crr.at[i])
        both = part[i, core].astype(F32) + cin[i].astype(F32)
        zb[i] = both.astype(BF).reshape(4, SEL, BLK)
        for d in range(1, 4):
            send(
                zb.at[i, lax.rem(zl + d, 4)], zin.at[i, d - 1],
                zrs.at[i, d - 1], zrr.at[i, d - 1], zl_dev(d),
            )

    def stage2(i):
        n = block(i)
        total = zb[i, zl].astype(F32)
        for d in range(1, 4):
            arrive(zin.at[i, d - 1], zrs.at[i, d - 1], zrr.at[i, d - 1])
            total = total + zin[i, d - 1].astype(F32)
        y[n, core, zl] = total.astype(BF)
        for d in range(1, 4):
            ref = y.at[n, core, zl]
            send(ref, ref, ags.at[i, d - 1], agr.at[i, d - 1], zl_dev(d))

    def stage3(i):
        n = block(i)
        for d in range(1, 4):
            arrive(y.at[n, core, lax.rem(zl + 4 - d, 4)], ags.at[i, d - 1], agr.at[i, d - 1])
        ref = y.at[n, core]
        send(ref, ref, cgs.at[i], cgr.at[i], other)

    def stage4(i):
        n = block(i)
        arrive(y.at[n, 1 - core], cgs.at[i], cgr.at[i])

    def y_block(i):
        return y[block(i)].reshape(TOK, BLK)

    first_rows = (
        lax.broadcasted_iota(jnp.int32, (SEL, BLK), 0)
        == lax.broadcasted_iota(jnp.int32, (SEL, BLK), 1)
    ).astype(F32).astype(BF)

    def pick_y(i):
        n = block(i)
        sely[n] = lax.dot_general(first_rows, y_block(i), NT, preferred_element_type=F32).astype(BF)

    def forward(blocks):
        total = None
        for i in blocks:
            n = block(i)
            term = lax.dot_general(y_block(i), w2g[n], NT, preferred_element_type=F32)
            total = term if total is None else total + term
        return total

    def prepare():
        keep_row = (ids[...] != 0).astype(F32)
        across = lax.broadcasted_iota(jnp.int32, (TOK, TOK), 0)
        along = lax.broadcasted_iota(jnp.int32, (TOK, TOK), 1)
        keep_col = jnp.sum(
            jnp.where(across == along, jnp.broadcast_to(keep_row, (TOK, TOK)), 0.0),
            axis=1, keepdims=True,
        )
        up[...] = (up[...].astype(F32) * keep_col).astype(BF)
        own_rows = (
            lax.broadcasted_iota(jnp.int32, (SEL, BLK), 0) + SEL * t
            == lax.broadcasted_iota(jnp.int32, (SEL, BLK), 1)
        ).astype(F32).astype(BF)
        stt[...] = lax.dot_general(own_rows, st[...], NT, preferred_element_type=F32) * keep_row
        pc1[...] = lax.dot_general(first_rows, w1g[r], NT, preferred_element_type=F32)
        pc2[...] = lax.dot_general(first_rows, w2g[c], NT, preferred_element_type=F32)

    stage0(0)
    prepare()
    stage1(0)
    stage2(0)
    for way in range(2):
        w1_wait(way, 0, 0)
        w1_send(way, 1, 0)
    for way in range(2):
        w2_wait(0, way, 0)
        w2_send(0, way, 2)
    stage3(0)
    for way in range(2):
        w1_wait(way, 0, 1)
        w1_send(way, 1, 1)
    stage0(1)
    stage0(2)
    for way in range(2):
        z_second(way)
    stage4(0)
    pick_y(0)
    stage1(1)
    stage1(2)
    for way in range(2):
        w2_wait(0, way, 1)
    for way in range(2):
        w1_wait(way, 1, 0)
        w1_send(way, 2, 0)
    stage2(1)
    stage2(2)
    for way in range(2):
        w2_wait(0, way, 2)
    stage3(1)
    stage3(2)
    for way in range(2):
        w1_wait(way, 1, 1)
        w1_send(way, 2, 1)
    stage0(3)
    stage0(4)
    stage4(1)
    stage4(2)
    pick_y(1)
    pick_y(2)
    stage1(3)
    stage1(4)
    for way in range(2):
        z_wait(way)
    for j in range(2):
        for way in range(2):
            w2_send(1, way, j)
    for way in range(2):
        w1_wait(way, 2, 0)
        w1_send(way, 3, 0)
    stage2(3)
    stage2(4)
    stage3(3)
    stage3(4)
    for way in range(2):
        w2_wait(1, way, 0)
        w2_send(1, way, 2)
    for way in range(2):
        w1_wait(way, 2, 1)
    stage0(5)
    stage0(6)
    stage4(3)
    stage4(4)
    pick_y(3)
    pick_y(4)
    stage1(5)
    stage1(6)
    for way in range(2):
        w1_wait(way, 3, 0)
    stage0(7)
    stage2(5)
    stage2(6)
    stage1(7)
    stage3(5)
    stage3(6)
    stage2(7)
    stage4(5)
    stage4(6)
    pick_y(5)
    pick_y(6)
    for way in range(2):
        w2_wait(1, way, 1)
    for way in range(2):
        w2_wait(1, way, 2)
    for n in range(8):
        selw[n] = lax.dot_general(first_rows, w2g[n], NT, preferred_element_type=F32).astype(BF)
    stage3(7)
    pre2[...] = forward(range(7))
    stage4(7)
    pick_y(7)

    last = block(7)
    y_last = y_block(7)
    carried = jnp.zeros((BLK, TOK), F32)
    for k in range(4):
        cols = slice(256 * k, 256 * k + 256)
        pre = pre2[:, cols] + lax.dot_general(
            y_last, w2g[last, cols], NT, preferred_element_type=F32
        )
        pre = pre * SCALE_MODEL
        squash = jax.nn.sigmoid(pre)
        piece = (up[:, cols].astype(F32) * squash * (1.0 + pre * (1.0 - squash))).astype(BF)
        slope[:, cols] = piece
        carried = carried + lax.dot_general(
            selw[:, :, cols].reshape(BLK, 256), piece, NT, preferred_element_type=F32
        )
    q[...] = (carried * SCALE_MODEL).astype(BF).reshape(8, SEL, TOK)
    for d in range(1, 8):
        send(q.at[lax.rem(t + d, 8)], qin.at[d - 1], qs.at[d - 1], qr.at[d - 1], tp_dev(d))

    factor = weight * INNER
    grad = jnp.dot(sely[...].reshape(BLK, TOK), slope[...], preferred_element_type=F32) * SCALE_MODEL
    t2[...] = (factor * grad).astype(BF).reshape(4, 2, SEL, HID)
    for d in range(1, 4):
        send(t2.at[lax.rem(x + d, 4)], t2x.at[d - 1], xs.at[d - 1], xr.at[d - 1], x_dev(d))

    total = q[t].astype(F32) + stt[...]
    for d in range(1, 8):
        arrive(qin.at[d - 1], qs.at[d - 1], qr.at[d - 1])
        total = total + qin[d - 1].astype(F32)
    dy[t] = total.astype(BF)
    for d in range(1, 8):
        ref = dy.at[t]
        send(ref, ref, ds_.at[d - 1], dr_.at[d - 1], tp_dev(d))
    for d in range(1, 8):
        arrive(dy.at[lax.rem(t + 8 - d, 8)], ds_.at[d - 1], dr_.at[d - 1])
    grad = jnp.dot(dy[...].reshape(BLK, TOK), act[...], preferred_element_type=F32) * SCALE_HIDDEN
    t1[...] = (factor * grad).astype(BF).reshape(8, SEL, HID)
    for d in (4, 3, 5, 2, 6, 1, 7):
        send(t1.at[lax.rem(r + d, 8)], t1in.at[d - 1], rs_.at[d - 1], rr_.at[d - 1], row_dev(d))

    far = t2[x, 1 - zh].astype(F32)
    near = t2[x, zh].astype(F32)
    for d in range(1, 4):
        arrive(t2x.at[d - 1], xs.at[d - 1], xr.at[d - 1])
        far = far + t2x[d - 1, 1 - zh].astype(F32)
        near = near + t2x[d - 1, zh].astype(F32)
    t2z[...] = far.astype(BF)
    send(t2z, t2zin, as_, ar_, antipode)

    def total_of(buffer, s_sems, r_sems):
        count = wown[...]
        for d in range(1, 8):
            arrive(buffer.at[d - 1], s_sems.at[d - 1], r_sems.at[d - 1])
            count = count + buffer[d - 1]
        return count[0:1, 0:1]

    total_one = total_of(wrow, nrs, nrr)
    total_two = total_of(wcol, ncs, ncr)

    arrive(t2zin, as_, ar_)
    delta = (near + t2zin[...].astype(F32)) / total_two
    moment = DECAY * m2[...] + delta
    n2[...] = moment
    o2[...] = pc2[...] - OUTER * (delta + DECAY * moment)

    summed = t1[r].astype(F32)
    for d in (1, 7, 2, 6, 3, 5, 4):
        arrive(t1in.at[d - 1], rs_.at[d - 1], rr_.at[d - 1])
        summed = summed + t1in[d - 1].astype(F32)
    delta = summed / total_one
    moment = DECAY * m1[...] + delta
    n1[...] = moment
    o1[...] = pc1[...] - OUTER * (delta + DECAY * moment)

    for copy in pending:
        copy.wait_send()


def on_device(
    act_one, residual, upstream, stream_grad, token_ids, shard_counts,
    out_one, in_two, out_one_moment, in_two_moment,
):
    dma = pltpu.SemaphoreType.DMA
    vmem = pltpu.VMEM
    whole = pl.BlockSpec(memory_space=pl.ANY)
    inside = pl.BlockSpec(memory_space=pltpu.VMEM)
    scratch = [
        vmem((TOK, HID), BF), vmem((TOK, BLK), BF), vmem((TOK, HID), BF), vmem((TOK, BLK), BF),
        vmem((1, TOK), jnp.int32), vmem((8, HID, BLK), BF), vmem((8, HID, BLK), BF),
        vmem((SEL, HID), F32), vmem((SEL, HID), F32),
        vmem((8, 2, 128, BLK), BF), vmem((8, 128, BLK), BF),
        vmem((8, 4, SEL, BLK), BF), vmem((8, 3, SEL, BLK), BF),
        vmem((8, 2, 4, SEL, BLK), BF), vmem((2, 512, BLK), BF),
        vmem((TOK, HID), F32), vmem((TOK, HID), BF), vmem((8, SEL, HID), BF),
        vmem((8, SEL, TOK), BF), vmem((SEL, TOK), F32), vmem((SEL, HID), F32), vmem((SEL, HID), F32),
        vmem((8, SEL, TOK), BF), vmem((7, SEL, TOK), BF), vmem((8, SEL, TOK), BF),
        vmem((8, SEL, HID), BF), vmem((7, SEL, HID), BF),
        vmem((4, 2, SEL, HID), BF), vmem((3, 2, SEL, HID), BF),
        vmem((SEL, HID), BF), vmem((SEL, HID), BF),
        vmem((8, 128), F32), vmem((7, 8, 128), F32), vmem((7, 8, 128), F32),
        dma((9,)),
        dma((2, 4, 2)), dma((2, 4, 2)), dma((2, 2, 3)), dma((2, 2, 3)), dma((2, 2)), dma((2, 2)),
        dma((8,)), dma((8,)), dma((8, 3)), dma((8, 3)), dma((8, 3)), dma((8, 3)), dma((8,)), dma((8,)),
        dma((7,)), dma((7,)), dma((7,)), dma((7,)), dma((7,)), dma((7,)),
        dma((3,)), dma((3,)), dma(()), dma(()), dma((7,)), dma((7,)), dma((7,)), dma((7,)),
    ]
    result = jax.ShapeDtypeStruct((SEL, HID), F32)
    o1, n1, o2, n2 = pl.pallas_call(
        kernel,
        out_shape=(result,) * 4,
        in_specs=[whole] * 5 + [inside] + [whole] * 4,
        out_specs=(inside,) * 4,
        scratch_shapes=scratch,
        compiler_params=pltpu.CompilerParams(
            collective_id=0, has_side_effects=True, vmem_limit_bytes=48 * 1024 * 1024
        ),
        cost_estimate=pl.CostEstimate(flops=3_000_000_000, bytes_accessed=4_000_000, transcendentals=300_000),
    )(
        act_one[0, 0], residual[0, 0], upstream[0, 0], stream_grad[0, 0], token_ids[0],
        shard_counts, out_one[0], in_two[0], out_one_moment[0].T, in_two_moment[0].T,
    )
    return (o1.T[None], n1.T[None], o2.T[None], n2.T[None])


def solution(mesh):
    return jax.shard_map(
        on_device,
        mesh=mesh,
        in_specs=(
            P("row", "col", None, "tp"),
            P("row", "col", None, "tp"),
            P("row", "col", None, "tp"),
            P("row", "col", None, None),
            P("row", "col", None),
            P("row", "col"),
            P("col", "tp", "row"),
            P("row", "tp", "col"),
            P("col", "tp", "row"),
            P("row", "tp", "col"),
        ),
        out_specs=(
            P("col", "tp", "row"),
            P("col", "tp", "row"),
            P("row", "tp", "col"),
            P("row", "tp", "col"),
        ),
        check_vma=False,
    )
```

```python
import math

import jax
import jax.numpy as jnp
from jax import lax
from jax.experimental import pallas as pl
from jax.experimental.pallas import tpu as pltpu
from jax.sharding import PartitionSpec as P

D = 2048
H = 8192
TOK = 256
HID = 1024
BLK = 256
SEL = 32
INNER = 4.0
OUTER = 0.7
DECAY = 0.9
MESH = pl.DeviceIdType.MESH
BF = jnp.bfloat16
F32 = jnp.float32

SCALE_MODEL = 1.0 / math.sqrt(D)
SCALE_HIDDEN = 1.0 / math.sqrt(H)
NT = (((1,), (1,)), ((), ()))
HALF = 128


def kernel(
    act_h, res_h, up_h, st_h, ids_h, cnt_v, w1_h, w2_h, m1_h, m2_h,
    o1, n1, o2, n2,
    act, res, up, st, ids, w1g, w2g, m1, m2,
    part, cin, zb, zin, y, relay, pre2, slope, selw, sely, stt, pc1, pc2,
    q, qin, dy, t1, t1in, t2, t2x, t2z, t2zin, wown, wrow, wcol,
    loc, w1s, w1r, w2s, w2r, zs, zr,
    crs, crr, zrs, zrr, ags, agr, cgs, cgr,
    qs, qr, ds_, dr_, rs_, rr_, xs, xr, as_, ar_, nrs, nrr, ncs, ncr,
):
    r = lax.axis_index("row")
    c = lax.axis_index("col")
    t = lax.axis_index("tp")
    x = lax.div(c, 2)
    zh = lax.rem(c, 2)
    zl = lax.div(t, 2)
    core = lax.rem(t, 2)
    z = zh * 4 + zl
    other = (r, c, zl * 2 + 1 - core)

    def row_dev(d):
        return (lax.rem(r + d, 8), c, t)

    def tp_dev(d):
        return (r, c, lax.rem(t + d, 8))

    def x_dev(d):
        return (r, lax.rem(x + d, 4) * 2 + zh, t)

    def z_dev(d):
        to = lax.rem(z + d, 8)
        return (r, x * 2 + lax.div(to, 4), lax.rem(to, 4) * 2 + core)

    def zl_dev(d):
        return (r, c, lax.rem(zl + d, 4) * 2 + core)

    def col_dev(d):
        return (r, lax.rem(c + d, 8), t)

    antipode = (r, x * 2 + 1 - zh, t)
    pending = []

    def send(src, dst, s_sem, r_sem, device):
        copy = pltpu.make_async_remote_copy(
            src_ref=src, dst_ref=dst, send_sem=s_sem, recv_sem=r_sem,
            device_id=device, device_id_type=MESH,
        )
        copy.start()
        pending.append(copy)

    def arrive(dst, s_sem, r_sem):
        pltpu.make_async_remote_copy(
            src_ref=dst, dst_ref=dst, send_sem=s_sem, recv_sem=r_sem,
            device_id=other, device_id_type=MESH,
        ).wait_recv()

    local = [
        pltpu.make_async_copy(a, b, loc.at[k])
        for k, (a, b) in enumerate(
            (
                (w1_h.at[:, pl.ds(0, HALF)], w1g.at[r, 0]), (w1_h.at[:, pl.ds(HALF, HALF)], w1g.at[r, 1]),
                (w2_h, w2g.at[c]), (act_h, act), (res_h, res),
                (up_h, up), (st_h, st), (ids_h, ids), (m1_h, m1), (m2_h, m2),
            )
        )
    ]
    for copy in local:
        copy.start()

    barrier = pltpu.get_barrier_semaphore()
    partners = (
        [row_dev(d) for d in range(1, 8)]
        + [col_dev(d) for d in range(1, 8)]
        + [tp_dev(d) for d in range(1, 8)]
        + [z_dev(2), z_dev(6)]
    )
    for device in partners:
        pl.semaphore_signal(barrier, inc=1, device_id=device, device_id_type=MESH)
    weight = cnt_v[...].astype(F32)
    wown[...] = jnp.broadcast_to(weight, (8, 128))
    pl.semaphore_wait(barrier, len(partners))

    def chunk(way, step, j):
        return lax.rem(r + (8 - step if way == 0 else step), 8), (j if way == 0 else 1 - j)

    def w1_send(way, step, j):
        ref = w1g.at[chunk(way, step, j)]
        send(ref, ref, w1s.at[way, step, j], w1r.at[way, step, j], row_dev(1 if way == 0 else 7))

    def ring(k):
        step, j = divmod(k - 1, 2)
        for way in range(2):
            arrive(w1g.at[chunk(way, step + 1, j)], w1s.at[way, step, j], w1r.at[way, step, j])
            if step < 2 or (step == 2 and j == 0):
                w1_send(way, step + 1, j)

    def w2_chunk(at, phase, half):
        plane = zh if phase == 0 else 1 - zh
        return w2g.at[lax.rem(at, 4) * 2 + plane, pl.ds(512 * half, 512)]

    def w2_send(phase, way, j):
        half = j % 2 if way == 0 else 1 - j % 2
        back = 0 if j < 2 else 1
        at = x + (4 - back if way == 0 else back)
        ref = w2_chunk(at, phase, half)
        send(ref, ref, w2s.at[phase, way, j], w2r.at[phase, way, j], x_dev(1 if way == 0 else 3))

    def w2_wait(phase, way, j):
        half = j % 2 if way == 0 else 1 - j % 2
        back = 1 if j < 2 else 2
        at = x + (4 - back if way == 0 else back)
        arrive(w2_chunk(at, phase, half), w2s.at[phase, way, j], w2r.at[phase, way, j])

    def z_first(way):
        send(
            w2g.at[c, pl.ds(512 * way, 512)], relay.at[way],
            zs.at[way, 0], zr.at[way, 0], z_dev(2 if way == 0 else 6),
        )

    def z_second(way):
        arrive(relay.at[way], zs.at[way, 0], zr.at[way, 0])
        hop = 2 if way == 0 else 6
        far = lax.div(lax.rem(z + hop, 8), 4)
        send(
            relay.at[way], w2g.at[x * 2 + 1 - far, pl.ds(512 * way, 512)],
            zs.at[way, 1], zr.at[way, 1], z_dev(hop),
        )

    def z_wait(way):
        arrive(w2g.at[x * 2 + 1 - zh, pl.ds(512 * way, 512)], zs.at[way, 1], zr.at[way, 1])

    local[0].wait()
    local[1].wait()
    for j in range(2):
        for way in range(2):
            w1_send(way, 0, j)
    local[2].wait()
    for j in range(2):
        for way in range(2):
            w2_send(0, way, j)
    for way in range(2):
        z_first(way)
    for copy in local[3:]:
        copy.wait()

    def send_counts():
        for d in range(1, 8):
            send(wown, wrow.at[d - 1], nrs.at[d - 1], nrr.at[d - 1], row_dev(d))
            send(wown, wcol.at[d - 1], ncs.at[d - 1], ncr.at[d - 1], col_dev(d))

    def group(g):
        step, j = (0, 0) if g == 0 else ((g + 1) // 2, (g - 1) % 2)
        first = chunk(0, step, j)
        second = chunk(1, step, j)
        return first, second

    def stage0(g):
        (na, ha), (nb, hb) = group(g)
        rhs = jnp.concatenate([w1g[na, ha], w1g[nb, hb]], axis=1)
        acc = jnp.dot(act[...], rhs, preferred_element_type=F32) * SCALE_HIDDEN
        own = []
        for n, half in ((na, ha), (nb, hb)):
            mine = jnp.where(n == t, 1.0, 0.0).astype(F32)
            own.append(res[:, HALF * half : HALF * half + HALF].astype(F32) * mine)
        acc = acc + jnp.concatenate(own, axis=1)
        part[g] = acc.astype(BF).reshape(2, 128, BLK)
        send(part.at[g, 1 - core], cin.at[g], crs.at[g], crr.at[g], other)

    def stage1(i):
        arrive(cin.at[i], crs.at[i], crr.at[i])
        both = part[i, core].astype(F32) + cin[i].astype(F32)
        zb[i] = both.astype(BF).reshape(4, SEL, BLK)
        for d in range(1, 4):
            send(
                zb.at[i, lax.rem(zl + d, 4)], zin.at[i, d - 1],
                zrs.at[i, d - 1], zrr.at[i, d - 1], zl_dev(d),
            )

    def stage2(i):
        total = zb[i, zl].astype(F32)
        for d in range(1, 4):
            arrive(zin.at[i, d - 1], zrs.at[i, d - 1], zrr.at[i, d - 1])
            total = total + zin[i, d - 1].astype(F32)
        y[i, core, zl] = total.astype(BF)
        for d in range(1, 4):
            ref = y.at[i, core, zl]
            send(ref, ref, ags.at[i, d - 1], agr.at[i, d - 1], zl_dev(d))

    def stage3(i):
        for d in range(1, 4):
            arrive(y.at[i, core, lax.rem(zl + 4 - d, 4)], ags.at[i, d - 1], agr.at[i, d - 1])
        ref = y.at[i, core]
        send(ref, ref, cgs.at[i], cgr.at[i], other)

    def stage4(i):
        arrive(y.at[i, 1 - core], cgs.at[i], cgr.at[i])

    def rows_at(start):
        return (
            lax.broadcasted_iota(jnp.int32, (SEL, BLK), 0) + start
            == lax.broadcasted_iota(jnp.int32, (SEL, BLK), 1)
        ).astype(F32).astype(BF)

    first_rows = rows_at(0)
    other_rows = rows_at(HALF)

    def y_group(g):
        return y[g].reshape(TOK, BLK)

    def back(step):
        return lax.rem(r + 8 - step, 8)

    def ahead(step):
        return lax.rem(r + step, 8)

    def pick_y(n, g, rows):
        sely[n] = lax.dot_general(rows, y_group(g), NT, preferred_element_type=F32).astype(BF)

    def pick_pair(step):
        pick_y(back(step), 2 * step - 1, first_rows)
        pick_y(ahead(step), 2 * step, other_rows)

    def pick_w(n):
        selw[n] = lax.dot_general(first_rows, w2g[n], NT, preferred_element_type=F32).astype(BF)

    def product(values, n):
        return lax.dot_general(values, w2g[n], NT, preferred_element_type=F32)

    def pair(step):
        low, high = y_group(2 * step - 1), y_group(2 * step)
        behind = jnp.concatenate([low[:, :HALF], high[:, :HALF]], axis=1)
        before = jnp.concatenate([high[:, HALF:], low[:, HALF:]], axis=1)
        return product(behind, back(step)) + product(before, ahead(step))

    def prepare():
        keep_row = (ids[...] != 0).astype(F32)
        across = lax.broadcasted_iota(jnp.int32, (TOK, TOK), 0)
        along = lax.broadcasted_iota(jnp.int32, (TOK, TOK), 1)
        keep_col = jnp.sum(
            jnp.where(across == along, jnp.broadcast_to(keep_row, (TOK, TOK)), 0.0),
            axis=1, keepdims=True,
        )
        up[...] = (up[...].astype(F32) * keep_col).astype(BF)
        stt[...] = lax.dot_general(rows_at(SEL * t), st[...], NT, preferred_element_type=F32) * keep_row
        pc1[...] = lax.dot_general(first_rows[:, :HALF], w1g[r, 0], NT, preferred_element_type=F32)
        pc2[...] = lax.dot_general(first_rows, w2g[c], NT, preferred_element_type=F32)

    stage0(0)
    prepare()
    stage1(0)

    ring(1)
    for way in range(2):
        w2_wait(0, way, 0)
        w2_send(0, way, 2)
    stage0(1)
    stage2(0)
    stage1(1)
    send_counts()

    ring(2)
    stage0(2)
    for way in range(2):
        z_second(way)
    stage2(1)
    stage3(0)
    stage1(2)
    for way in range(2):
        w2_wait(0, way, 1)
    stage4(0)
    pick_y(r, 0, first_rows)

    ring(3)
    stage0(3)
    stage2(2)
    stage3(1)
    stage1(3)
    stage4(1)
    for way in range(2):
        w2_wait(0, way, 2)

    ring(4)
    stage0(4)
    stage2(3)
    stage3(2)
    stage1(4)
    stage4(2)
    for way in range(2):
        z_wait(way)
    for j in range(2):
        for way in range(2):
            w2_send(1, way, j)
    pick_pair(1)
    for k in range(4):
        pick_w(2 * k + zh)

    ring(5)
    stage0(5)
    stage2(4)
    stage3(3)
    stage1(5)
    stage4(3)
    for way in range(2):
        w2_wait(1, way, 0)
        w2_send(1, way, 2)

    ring(6)
    stage0(6)
    stage2(5)
    stage3(4)
    stage1(6)
    stage4(4)
    pick_pair(2)

    ring(7)
    stage0(7)
    stage2(6)
    stage1(7)
    stage3(5)
    stage4(5)
    for way in range(2):
        w2_wait(1, way, 1)
        w2_wait(1, way, 2)
    for k in range(4):
        pick_w(2 * k + 1 - zh)
    stage3(6)
    pre2[...] = product(y_group(0), r) + pair(1)
    stage2(7)
    stage4(6)
    pre2[...] += pair(2)
    pick_pair(3)
    pre2[...] += pair(3)
    stage3(7)
    stage4(7)

    last = ahead(4)
    y_last = y_group(7)
    carried = jnp.zeros((BLK, TOK), F32)
    for k in range(4):
        cols = slice(256 * k, 256 * k + 256)
        pre = pre2[:, cols] + lax.dot_general(
            y_last, w2g[last, cols], NT, preferred_element_type=F32
        )
        pre = pre * SCALE_MODEL
        squash = jax.nn.sigmoid(pre)
        piece = (up[:, cols].astype(F32) * squash * (1.0 + pre * (1.0 - squash))).astype(BF)
        slope[:, cols] = piece
        carried = carried + lax.dot_general(
            selw[:, :, cols].reshape(BLK, 256), piece, NT, preferred_element_type=F32
        )
    q[...] = (carried * SCALE_MODEL).astype(BF).reshape(8, SEL, TOK)
    for d in range(1, 8):
        send(q.at[lax.rem(t + d, 8)], qin.at[d - 1], qs.at[d - 1], qr.at[d - 1], tp_dev(d))

    pick_y(last, 7, first_rows)
    factor = weight * INNER
    grad = jnp.dot(sely[...].reshape(BLK, TOK), slope[...], preferred_element_type=F32) * SCALE_MODEL
    t2[...] = (factor * grad).astype(BF).reshape(4, 2, SEL, HID)
    for d in range(1, 4):
        send(t2.at[lax.rem(x + d, 4)], t2x.at[d - 1], xs.at[d - 1], xr.at[d - 1], x_dev(d))

    total = q[t].astype(F32) + stt[...]
    for d in range(1, 8):
        arrive(qin.at[d - 1], qs.at[d - 1], qr.at[d - 1])
        total = total + qin[d - 1].astype(F32)
    dy[t] = total.astype(BF)
    for d in range(1, 8):
        ref = dy.at[t]
        send(ref, ref, ds_.at[d - 1], dr_.at[d - 1], tp_dev(d))
    for d in range(1, 8):
        arrive(dy.at[lax.rem(t + 8 - d, 8)], ds_.at[d - 1], dr_.at[d - 1])
    grad = jnp.dot(dy[...].reshape(BLK, TOK), act[...], preferred_element_type=F32) * SCALE_HIDDEN
    t1[...] = (factor * grad).astype(BF).reshape(8, SEL, HID)

    def row_send(d):
        send(t1.at[lax.rem(r + d, 8)], t1in.at[d - 1], rs_.at[d - 1], rr_.at[d - 1], row_dev(d))

    joint = jnp.where(core == 0, 5, 3)
    send(t1.at[lax.rem(r + 4, 8)], t1in.at[3], rs_.at[3], rr_.at[3], row_dev(jnp.where(core == 0, 7, 1)))
    row_send(8 - joint)
    for d in (2, 6, 1, 7):
        row_send(d)

    far = t2[x, 1 - zh].astype(F32)
    near = t2[x, zh].astype(F32)
    for d in range(1, 4):
        arrive(t2x.at[d - 1], xs.at[d - 1], xr.at[d - 1])
        far = far + t2x[d - 1, 1 - zh].astype(F32)
        near = near + t2x[d - 1, zh].astype(F32)
    t2z[...] = far.astype(BF)
    send(t2z, t2zin, as_, ar_, antipode)

    arrive(t1in.at[3], rs_.at[3], rr_.at[3])
    to = lax.rem(r + joint, 8)
    t1[to] = (t1[to].astype(F32) + t1in[3].astype(F32)).astype(BF)
    row_send(joint)

    def total_of(buffer, s_sems, r_sems):
        count = wown[...]
        for d in range(1, 8):
            arrive(buffer.at[d - 1], s_sems.at[d - 1], r_sems.at[d - 1])
            count = count + buffer[d - 1]
        return count[0:1, 0:1]

    total_one = total_of(wrow, nrs, nrr)
    total_two = total_of(wcol, ncs, ncr)

    arrive(t2zin, as_, ar_)
    delta = (near + t2zin[...].astype(F32)) / total_two
    moment = DECAY * m2[...] + delta
    n2[...] = moment
    o2[...] = pc2[...] - OUTER * (delta + DECAY * moment)

    summed = t1[r].astype(F32)
    for d in (1, 7, 2, 6, 3, 5):
        arrive(t1in.at[d - 1], rs_.at[d - 1], rr_.at[d - 1])
        summed = summed + t1in[d - 1].astype(F32)
    delta = summed / total_one
    moment = DECAY * m1[...] + delta
    n1[...] = moment
    o1[...] = pc1[...] - OUTER * (delta + DECAY * moment)

    for copy in pending:
        copy.wait_send()


def in_hbm(value):
    return pltpu.with_memory_space_constraint(value, pltpu.HBM)


def on_device(
    act_one, residual, upstream, stream_grad, token_ids, shard_counts,
    out_one, in_two, out_one_moment, in_two_moment,
):
    dma = pltpu.SemaphoreType.DMA
    vmem = pltpu.VMEM
    whole = pl.BlockSpec(memory_space=pltpu.HBM)
    inside = pl.BlockSpec(memory_space=pltpu.VMEM)
    scratch = [
        vmem((TOK, HID), BF), vmem((TOK, BLK), BF), vmem((TOK, HID), BF), vmem((TOK, BLK), BF),
        vmem((1, TOK), jnp.int32), vmem((8, 2, HID, HALF), BF), vmem((8, HID, BLK), BF),
        vmem((SEL, HID), F32), vmem((SEL, HID), F32),
        vmem((8, 2, 128, BLK), BF), vmem((8, 128, BLK), BF),
        vmem((8, 4, SEL, BLK), BF), vmem((8, 3, SEL, BLK), BF),
        vmem((8, 2, 4, SEL, BLK), BF), vmem((2, 512, BLK), BF),
        vmem((TOK, HID), F32), vmem((TOK, HID), BF), vmem((8, SEL, HID), BF),
        vmem((8, SEL, TOK), BF), vmem((SEL, TOK), F32), vmem((SEL, HID), F32), vmem((SEL, HID), F32),
        vmem((8, SEL, TOK), BF), vmem((7, SEL, TOK), BF), vmem((8, SEL, TOK), BF),
        vmem((8, SEL, HID), BF), vmem((7, SEL, HID), BF),
        vmem((4, 2, SEL, HID), BF), vmem((3, 2, SEL, HID), BF),
        vmem((SEL, HID), BF), vmem((SEL, HID), BF),
        vmem((8, 128), F32), vmem((7, 8, 128), F32), vmem((7, 8, 128), F32),
        dma((10,)),
        dma((2, 4, 2)), dma((2, 4, 2)), dma((2, 2, 3)), dma((2, 2, 3)), dma((2, 2)), dma((2, 2)),
        dma((8,)), dma((8,)), dma((8, 3)), dma((8, 3)), dma((8, 3)), dma((8, 3)), dma((8,)), dma((8,)),
        dma((7,)), dma((7,)), dma((7,)), dma((7,)), dma((7,)), dma((7,)),
        dma((3,)), dma((3,)), dma(()), dma(()), dma((7,)), dma((7,)), dma((7,)), dma((7,)),
    ]
    result = jax.ShapeDtypeStruct((SEL, HID), F32)
    o1, n1, o2, n2 = pl.pallas_call(
        kernel,
        out_shape=(result,) * 4,
        in_specs=[whole] * 5 + [inside] + [whole] * 4,
        out_specs=(inside,) * 4,
        scratch_shapes=scratch,
        compiler_params=pltpu.CompilerParams(
            collective_id=0, has_side_effects=True, vmem_limit_bytes=48 * 1024 * 1024
        ),
        cost_estimate=pl.CostEstimate(flops=3_000_000_000, bytes_accessed=4_000_000, transcendentals=300_000),
    )(
        *map(in_hbm, (act_one[0, 0], residual[0, 0], upstream[0, 0], stream_grad[0, 0], token_ids[0])),
        shard_counts,
        *map(in_hbm, (out_one[0], in_two[0], out_one_moment[0].T, in_two_moment[0].T)),
    )
    return (o1.T[None], n1.T[None], o2.T[None], n2.T[None])


def solution(mesh):
    return jax.shard_map(
        on_device,
        mesh=mesh,
        in_specs=(
            P("row", "col", None, "tp"),
            P("row", "col", None, "tp"),
            P("row", "col", None, "tp"),
            P("row", "col", None, None),
            P("row", "col", None),
            P("row", "col"),
            P("col", "tp", "row"),
            P("row", "tp", "col"),
            P("col", "tp", "row"),
            P("row", "tp", "col"),
        ),
        out_specs=(
            P("col", "tp", "row"),
            P("col", "tp", "row"),
            P("row", "tp", "col"),
            P("row", "tp", "col"),
        ),
        check_vma=False,
    )
```

```python
import math

import jax
import jax.numpy as jnp
from jax import lax
from jax.experimental import pallas as pl
from jax.experimental.pallas import tpu as pltpu
from jax.sharding import PartitionSpec as P

D = 2048
H = 8192
TOK = 256
HID = 1024
BLK = 256
SEL = 32
INNER = 4.0
OUTER = 0.7
DECAY = 0.9
MESH = pl.DeviceIdType.MESH
BF = jnp.bfloat16
F32 = jnp.float32

SCALE_MODEL = 1.0 / math.sqrt(D)
SCALE_HIDDEN = 1.0 / math.sqrt(H)
NT = (((1,), (1,)), ((), ()))
HALF = 128


def kernel(
    act_h, res_h, up_h, st_h, ids_h, cnt_v, w1_h, w2_h, m1_h, m2_h,
    o1, n1, o2, n2,
    act, res, up, st, ids, w1g, w2g, m1, m2,
    part, cin, lin, zb, zin, y, relay, pre2, slope, selw, sely, stt, pc1, pc2,
    q, qin, dy, t1, t1in, t2, t2x, t2z, t2zin, wown, wrow, wcol,
    loc, w1s, w1r, w2s, w2r, zs, zr,
    crs, crr, zrs, zrr, ags, agr, cgs, cgr, lrs, lrr, lgs, lgr,
    qs, qr, ds_, dr_, rs_, rr_, xs, xr, as_, ar_, nrs, nrr, ncs, ncr,
):
    r = lax.axis_index("row")
    c = lax.axis_index("col")
    t = lax.axis_index("tp")
    x = lax.div(c, 2)
    zh = lax.rem(c, 2)
    zl = lax.div(t, 2)
    core = lax.rem(t, 2)
    z = zh * 4 + zl
    other = (r, c, zl * 2 + 1 - core)

    def row_dev(d):
        return (lax.rem(r + d, 8), c, t)

    def tp_dev(d):
        return (r, c, lax.rem(t + d, 8))

    def x_dev(d):
        return (r, lax.rem(x + d, 4) * 2 + zh, t)

    def z_dev(d):
        to = lax.rem(z + d, 8)
        return (r, x * 2 + lax.div(to, 4), lax.rem(to, 4) * 2 + core)

    def zl_dev(d):
        return (r, c, lax.rem(zl + d, 4) * 2 + core)

    def col_dev(d):
        return (r, lax.rem(c + d, 8), t)

    antipode = (r, x * 2 + 1 - zh, t)
    pending = []

    def send(src, dst, s_sem, r_sem, device):
        copy = pltpu.make_async_remote_copy(
            src_ref=src, dst_ref=dst, send_sem=s_sem, recv_sem=r_sem,
            device_id=device, device_id_type=MESH,
        )
        copy.start()
        pending.append(copy)

    def arrive(dst, s_sem, r_sem):
        pltpu.make_async_remote_copy(
            src_ref=dst, dst_ref=dst, send_sem=s_sem, recv_sem=r_sem,
            device_id=other, device_id_type=MESH,
        ).wait_recv()

    local = [
        pltpu.make_async_copy(a, b, loc.at[k])
        for k, (a, b) in enumerate(
            (
                (w1_h.at[:, pl.ds(0, HALF)], w1g.at[r, 0]), (w1_h.at[:, pl.ds(HALF, HALF)], w1g.at[r, 1]),
                (w2_h, w2g.at[c]), (act_h, act), (res_h, res),
                (up_h, up), (st_h, st), (ids_h, ids), (m1_h, m1), (m2_h, m2),
            )
        )
    ]
    for copy in local:
        copy.start()

    barrier = pltpu.get_barrier_semaphore()
    partners = [row_dev(1), row_dev(7), x_dev(1), x_dev(3), z_dev(2), z_dev(6), other]
    partners += [zl_dev(d) for d in range(1, 4)]
    for device in partners:
        pl.semaphore_signal(barrier, inc=1, device_id=device, device_id_type=MESH)
    pl.semaphore_wait(barrier, len(partners))

    def chunk(way, step, j):
        return lax.rem(r + (8 - step if way == 0 else step), 8), (j if way == 0 else 1 - j)

    def w1_send(way, step, j):
        ref = w1g.at[chunk(way, step, j)]
        send(ref, ref, w1s.at[way, step, j], w1r.at[way, step, j], row_dev(1 if way == 0 else 7))

    def ring(k):
        step, j = divmod(k - 1, 2)
        for way in range(2):
            arrive(w1g.at[chunk(way, step + 1, j)], w1s.at[way, step, j], w1r.at[way, step, j])
            if step < 2 or (step == 2 and j == 0):
                w1_send(way, step + 1, j)

    def near_half(at, half):
        return w2g.at[lax.rem(at, 4) * 2 + zh, pl.ds(512 * half, 512)]

    def far_quarter(at, quarter):
        return w2g.at[lax.rem(at, 4) * 2 + 1 - zh, pl.ds(256 * quarter, 256)]

    def near_part(way, e, hops):
        half = (0, 1, 0)[e] if way == 0 else (1, 0, 1)[e]
        steps = hops + (1 if e == 2 else 0)
        return near_half(x + (4 - steps if way == 0 else steps), half)

    def far_part(way, e, hops):
        quarter = (0, 2, 1, 3, 0, 1)[e] if way == 0 else (2, 0, 3, 1, 2, 3)[e]
        steps = hops + (1 if e > 3 else 0)
        return far_quarter(x + (4 - steps if way == 0 else steps), quarter)

    def near_send(way, e):
        ref = near_part(way, e, 0)
        send(ref, ref, w2s.at[way, e], w2r.at[way, e], x_dev(1 if way == 0 else 3))

    def near_wait(way, e):
        arrive(near_part(way, e, 1), w2s.at[way, e], w2r.at[way, e])

    def far_send(way, e):
        ref = far_part(way, e, 0)
        send(ref, ref, w2s.at[way, 3 + e], w2r.at[way, 3 + e], x_dev(1 if way == 0 else 3))

    def far_wait(way, e):
        arrive(far_part(way, e, 1), w2s.at[way, 3 + e], w2r.at[way, 3 + e])

    def z_first(way, e):
        send(
            w2g.at[c, pl.ds(512 * way + 256 * e, 256)], relay.at[way, e],
            zs.at[way, e, 0], zr.at[way, e, 0], z_dev(2 if way == 0 else 6),
        )

    def z_second(way, e):
        arrive(relay.at[way, e], zs.at[way, e, 0], zr.at[way, e, 0])
        hop = 2 if way == 0 else 6
        far = lax.div(lax.rem(z + hop, 8), 4)
        send(
            relay.at[way, e], w2g.at[x * 2 + 1 - far, pl.ds(512 * way + 256 * e, 256)],
            zs.at[way, e, 1], zr.at[way, e, 1], z_dev(hop),
        )

    def z_wait(way, e):
        arrive(far_quarter(x, 2 * way + e), zs.at[way, e, 1], zr.at[way, e, 1])

    local[0].wait()
    local[1].wait()
    for j in range(2):
        for way in range(2):
            w1_send(way, 0, j)
    local[2].wait()
    for e in range(2):
        for way in range(2):
            z_first(way, e)
            near_send(way, e)
    for copy in local[3:]:
        copy.wait()

    weight = cnt_v[...].astype(F32)
    wown[...] = jnp.broadcast_to(weight, (8, 128))

    def send_counts():
        for d in range(1, 8):
            send(wown, wrow.at[d - 1], nrs.at[d - 1], nrr.at[d - 1], row_dev(d))
            send(wown, wcol.at[d - 1], ncs.at[d - 1], ncr.at[d - 1], col_dev(d))

    def group(g):
        step, j = (0, 0) if g == 0 else ((g + 1) // 2, (g - 1) % 2)
        first = chunk(0, step, j)
        second = chunk(1, step, j)
        return first, second

    def partial_sum(g):
        (na, ha), (nb, hb) = group(g)
        rhs = jnp.concatenate([w1g[na, ha], w1g[nb, hb]], axis=1)
        acc = jnp.dot(act[...], rhs, preferred_element_type=F32) * SCALE_HIDDEN
        own = []
        for n, half in ((na, ha), (nb, hb)):
            mine = jnp.where(n == t, 1.0, 0.0).astype(F32)
            own.append(res[:, HALF * half : HALF * half + HALF].astype(F32) * mine)
        acc = acc + jnp.concatenate(own, axis=1)
        part[g] = acc.astype(BF).reshape(2, 4, SEL, BLK)

    def stage0(g):
        partial_sum(g)
        send(part.at[g, 1 - core], cin.at[g], crs.at[g], crr.at[g], other)

    def stage1(i):
        arrive(cin.at[i], crs.at[i], crr.at[i])
        both = part[i, core].astype(F32) + cin[i].astype(F32)
        zb[i] = both.astype(BF)
        for d in range(1, 4):
            send(
                zb.at[i, lax.rem(zl + d, 4)], zin.at[i, d - 1],
                zrs.at[i, d - 1], zrr.at[i, d - 1], zl_dev(d),
            )

    def stage2(i):
        total = zb[i, zl].astype(F32)
        for d in range(1, 4):
            arrive(zin.at[i, d - 1], zrs.at[i, d - 1], zrr.at[i, d - 1])
            total = total + zin[i, d - 1].astype(F32)
        y[i, core, zl] = total.astype(BF)
        for d in range(1, 4):
            ref = y.at[i, core, zl]
            send(ref, ref, ags.at[i, d - 1], agr.at[i, d - 1], zl_dev(d))

    def stage3(i):
        for d in range(1, 4):
            arrive(y.at[i, core, lax.rem(zl + 4 - d, 4)], ags.at[i, d - 1], agr.at[i, d - 1])
        ref = y.at[i, core]
        send(ref, ref, cgs.at[i], cgr.at[i], other)

    def stage4(i):
        arrive(y.at[i, 1 - core], cgs.at[i], cgr.at[i])

    def place(d):
        at = lax.rem(t + d, 8)
        return lax.rem(at, 2), lax.div(at, 2)

    def last_out():
        partial_sum(7)
        for d in range(1, 8):
            send(part.at[(7, *place(d))], lin.at[d - 1], lrs.at[d - 1], lrr.at[d - 1], tp_dev(d))

    def last_back():
        total = part[7, core, zl].astype(F32)
        for d in range(1, 8):
            arrive(lin.at[d - 1], lrs.at[d - 1], lrr.at[d - 1])
            total = total + lin[d - 1].astype(F32)
        y[7, core, zl] = total.astype(BF)
        for d in range(1, 8):
            ref = y.at[7, core, zl]
            send(ref, ref, lgs.at[d - 1], lgr.at[d - 1], tp_dev(d))

    def last_wait():
        for d in range(1, 8):
            arrive(y.at[(7, *place(8 - d))], lgs.at[d - 1], lgr.at[d - 1])

    def rows_at(start):
        return (
            lax.broadcasted_iota(jnp.int32, (SEL, BLK), 0) + start
            == lax.broadcasted_iota(jnp.int32, (SEL, BLK), 1)
        ).astype(F32).astype(BF)

    first_rows = rows_at(0)
    other_rows = rows_at(HALF)

    def y_group(g):
        return y[g].reshape(TOK, BLK)

    def back(step):
        return lax.rem(r + 8 - step, 8)

    def ahead(step):
        return lax.rem(r + step, 8)

    def pick_y(n, g, rows):
        sely[n] = lax.dot_general(rows, y_group(g), NT, preferred_element_type=F32).astype(BF)

    def pick_pair(step):
        pick_y(back(step), 2 * step - 1, first_rows)
        pick_y(ahead(step), 2 * step, other_rows)

    def pick_w(n):
        selw[n] = lax.dot_general(first_rows, w2g[n], NT, preferred_element_type=F32).astype(BF)

    def product(values, n):
        return lax.dot_general(values, w2g[n], NT, preferred_element_type=F32)

    def pair(step):
        low, high = y_group(2 * step - 1), y_group(2 * step)
        behind = jnp.concatenate([low[:, :HALF], high[:, :HALF]], axis=1)
        before = jnp.concatenate([high[:, HALF:], low[:, HALF:]], axis=1)
        return product(behind, back(step)) + product(before, ahead(step))

    def prepare():
        keep_row = (ids[...] != 0).astype(F32)
        across = lax.broadcasted_iota(jnp.int32, (TOK, TOK), 0)
        along = lax.broadcasted_iota(jnp.int32, (TOK, TOK), 1)
        keep_col = jnp.sum(
            jnp.where(across == along, jnp.broadcast_to(keep_row, (TOK, TOK)), 0.0),
            axis=1, keepdims=True,
        )
        up[...] = (up[...].astype(F32) * keep_col).astype(BF)
        stt[...] = lax.dot_general(rows_at(SEL * t), st[...], NT, preferred_element_type=F32) * keep_row
        pc1[...] = lax.dot_general(first_rows[:, :HALF], w1g[r, 0], NT, preferred_element_type=F32)
        pc2[...] = lax.dot_general(first_rows, w2g[c], NT, preferred_element_type=F32)

    stage0(0)
    prepare()
    stage1(0)

    ring(1)
    for way in range(2):
        z_second(way, 0)
    for way in range(2):
        near_wait(way, 0)
        near_send(way, 2)
    stage0(1)
    stage1(1)

    ring(2)
    for way in range(2):
        z_second(way, 1)
    stage0(2)
    stage2(0)
    stage1(2)
    for way in range(2):
        near_wait(way, 1)

    ring(3)
    stage0(3)
    stage2(1)
    stage1(3)
    for way in range(2):
        near_wait(way, 2)
    for k in range(4):
        pick_w(2 * k + zh)
    for way in range(2):
        z_wait(way, 0)
    for e in range(2):
        for way in range(2):
            far_send(way, e)

    ring(4)
    stage0(4)
    stage2(2)
    stage3(0)
    stage1(4)
    stage4(0)
    pick_y(r, 0, first_rows)
    for way in range(2):
        z_wait(way, 1)
    for e in range(2, 4):
        for way in range(2):
            far_send(way, e)

    ring(5)
    for way in range(2):
        far_wait(way, 0)
        far_send(way, 4)
    stage0(5)
    stage2(3)
    stage3(1)
    stage1(5)
    stage4(1)

    ring(6)
    for way in range(2):
        far_wait(way, 2)
        far_send(way, 5)
    stage0(6)
    stage2(4)
    stage3(2)
    stage1(6)
    stage2(5)
    stage4(2)
    pick_pair(1)

    ring(7)
    last_out()
    stage2(6)
    stage3(3)
    stage3(4)
    stage4(3)
    stage4(4)
    pick_pair(2)
    stage3(5)
    for way in range(2):
        for e in (1, 3, 4, 5):
            far_wait(way, e)
    send_counts()
    stage3(6)
    last_back()
    for k in range(4):
        pick_w(2 * k + 1 - zh)
    pre2[...] = product(y_group(0), r) + pair(1)
    pre2[...] += pair(2)
    stage4(5)
    stage4(6)
    pre2[...] += pair(3)
    pick_pair(3)
    last_wait()

    last = ahead(4)
    y_last = y_group(7)
    carried = jnp.zeros((BLK, TOK), F32)
    for k in range(4):
        cols = slice(256 * k, 256 * k + 256)
        pre = pre2[:, cols] + lax.dot_general(
            y_last, w2g[last, cols], NT, preferred_element_type=F32
        )
        pre = pre * SCALE_MODEL
        squash = jax.nn.sigmoid(pre)
        piece = (up[:, cols].astype(F32) * squash * (1.0 + pre * (1.0 - squash))).astype(BF)
        slope[:, cols] = piece
        carried = carried + lax.dot_general(
            selw[:, :, cols].reshape(BLK, 256), piece, NT, preferred_element_type=F32
        )
    q[...] = (carried * SCALE_MODEL).astype(BF).reshape(8, SEL, TOK)
    for d in range(1, 8):
        send(q.at[lax.rem(t + d, 8)], qin.at[d - 1], qs.at[d - 1], qr.at[d - 1], tp_dev(d))

    pick_y(last, 7, first_rows)
    factor = weight * INNER
    grad = jnp.dot(sely[...].reshape(BLK, TOK), slope[...], preferred_element_type=F32) * SCALE_MODEL
    t2[...] = (factor * grad).astype(BF).reshape(4, 2, SEL, HID)
    for d in range(1, 4):
        send(t2.at[lax.rem(x + d, 4)], t2x.at[d - 1], xs.at[d - 1], xr.at[d - 1], x_dev(d))

    total = q[t].astype(F32) + stt[...]
    for d in range(1, 8):
        arrive(qin.at[d - 1], qs.at[d - 1], qr.at[d - 1])
        total = total + qin[d - 1].astype(F32)
    dy[t] = total.astype(BF)
    for d in range(1, 8):
        ref = dy.at[t]
        send(ref, ref, ds_.at[d - 1], dr_.at[d - 1], tp_dev(d))
    for d in range(1, 8):
        arrive(dy.at[lax.rem(t + 8 - d, 8)], ds_.at[d - 1], dr_.at[d - 1])
    grad = jnp.dot(dy[...].reshape(BLK, TOK), act[...], preferred_element_type=F32) * SCALE_HIDDEN
    t1[...] = (factor * grad).astype(BF).reshape(8, SEL, HID)

    def row_send(d):
        send(t1.at[lax.rem(r + d, 8)], t1in.at[d - 1], rs_.at[d - 1], rr_.at[d - 1], row_dev(d))

    joint = jnp.where(core == 0, 5, 3)
    send(t1.at[lax.rem(r + 4, 8)], t1in.at[3], rs_.at[3], rr_.at[3], row_dev(jnp.where(core == 0, 7, 1)))
    row_send(8 - joint)
    for d in (2, 6, 1, 7):
        row_send(d)

    far = t2[x, 1 - zh].astype(F32)
    near = t2[x, zh].astype(F32)
    for d in range(1, 4):
        arrive(t2x.at[d - 1], xs.at[d - 1], xr.at[d - 1])
        far = far + t2x[d - 1, 1 - zh].astype(F32)
        near = near + t2x[d - 1, zh].astype(F32)
    t2z[...] = far.astype(BF)
    send(t2z, t2zin, as_, ar_, antipode)

    arrive(t1in.at[3], rs_.at[3], rr_.at[3])
    to = lax.rem(r + joint, 8)
    t1[to] = (t1[to].astype(F32) + t1in[3].astype(F32)).astype(BF)
    row_send(joint)

    def total_of(buffer, s_sems, r_sems):
        count = wown[...]
        for d in range(1, 8):
            arrive(buffer.at[d - 1], s_sems.at[d - 1], r_sems.at[d - 1])
            count = count + buffer[d - 1]
        return count[0:1, 0:1]

    total_one = total_of(wrow, nrs, nrr)
    total_two = total_of(wcol, ncs, ncr)

    arrive(t2zin, as_, ar_)
    delta = (near + t2zin[...].astype(F32)) / total_two
    moment = DECAY * m2[...] + delta
    n2[...] = moment
    o2[...] = pc2[...] - OUTER * (delta + DECAY * moment)

    summed = t1[r].astype(F32)
    for d in (1, 7, 2, 6, 3, 5):
        arrive(t1in.at[d - 1], rs_.at[d - 1], rr_.at[d - 1])
        summed = summed + t1in[d - 1].astype(F32)
    delta = summed / total_one
    moment = DECAY * m1[...] + delta
    n1[...] = moment
    o1[...] = pc1[...] - OUTER * (delta + DECAY * moment)

    for copy in pending:
        copy.wait_send()


def write_out(a, b, c, d, a_out, b_out, c_out, d_out, sems):
    copies = [
        pltpu.make_async_copy(src, dst, sems.at[k])
        for k, (src, dst) in enumerate(((a, a_out), (b, b_out), (c, c_out), (d, d_out)))
    ]
    for copy in copies:
        copy.start()
    for copy in copies:
        copy.wait()


def in_hbm(value):
    return pltpu.with_memory_space_constraint(value, pltpu.HBM)


def on_device(
    act_one, residual, upstream, stream_grad, token_ids, shard_counts,
    out_one, in_two, out_one_moment, in_two_moment,
):
    dma = pltpu.SemaphoreType.DMA
    vmem = pltpu.VMEM
    whole = pl.BlockSpec(memory_space=pltpu.HBM)
    inside = pl.BlockSpec(memory_space=pltpu.VMEM)
    scratch = [
        vmem((TOK, HID), BF), vmem((TOK, BLK), BF), vmem((TOK, HID), BF), vmem((TOK, BLK), BF),
        vmem((1, TOK), jnp.int32), vmem((8, 2, HID, HALF), BF), vmem((8, HID, BLK), BF),
        vmem((SEL, HID), F32), vmem((SEL, HID), F32),
        vmem((8, 2, 4, SEL, BLK), BF), vmem((7, 4, SEL, BLK), BF), vmem((7, SEL, BLK), BF),
        vmem((7, 4, SEL, BLK), BF), vmem((7, 3, SEL, BLK), BF),
        vmem((8, 2, 4, SEL, BLK), BF), vmem((2, 2, BLK, BLK), BF),
        vmem((TOK, HID), F32), vmem((TOK, HID), BF), vmem((8, SEL, HID), BF),
        vmem((8, SEL, TOK), BF), vmem((SEL, TOK), F32), vmem((SEL, HID), F32), vmem((SEL, HID), F32),
        vmem((8, SEL, TOK), BF), vmem((7, SEL, TOK), BF), vmem((8, SEL, TOK), BF),
        vmem((8, SEL, HID), BF), vmem((7, SEL, HID), BF),
        vmem((4, 2, SEL, HID), BF), vmem((3, 2, SEL, HID), BF),
        vmem((SEL, HID), BF), vmem((SEL, HID), BF),
        vmem((8, 128), F32), vmem((7, 8, 128), F32), vmem((7, 8, 128), F32),
        dma((10,)),
        dma((2, 4, 2)), dma((2, 4, 2)), dma((2, 9)), dma((2, 9)), dma((2, 2, 2)), dma((2, 2, 2)),
        dma((7,)), dma((7,)), dma((7, 3)), dma((7, 3)), dma((7, 3)), dma((7, 3)), dma((7,)), dma((7,)),
        dma((7,)), dma((7,)), dma((7,)), dma((7,)),
        dma((7,)), dma((7,)), dma((7,)), dma((7,)), dma((7,)), dma((7,)),
        dma((3,)), dma((3,)), dma(()), dma(()), dma((7,)), dma((7,)), dma((7,)), dma((7,)),
    ]
    result = jax.ShapeDtypeStruct((SEL, HID), F32)
    o1, n1, o2, n2 = pl.pallas_call(
        kernel,
        out_shape=(result,) * 4,
        in_specs=[whole] * 5 + [inside] + [whole] * 4,
        out_specs=(inside,) * 4,
        scratch_shapes=scratch,
        compiler_params=pltpu.CompilerParams(
            collective_id=0, has_side_effects=True, vmem_limit_bytes=48 * 1024 * 1024
        ),
        cost_estimate=pl.CostEstimate(flops=3_000_000_000, bytes_accessed=4_000_000, transcendentals=300_000),
    )(
        *map(in_hbm, (act_one[0, 0], residual[0, 0], upstream[0, 0], stream_grad[0, 0], token_ids[0])),
        shard_counts,
        *map(in_hbm, (out_one[0], in_two[0], out_one_moment[0].T, in_two_moment[0].T)),
    )
    o1, n1, o2, n2 = pl.pallas_call(
        write_out,
        out_shape=(result,) * 4,
        in_specs=[pl.BlockSpec(memory_space=pl.ANY)] * 4,
        out_specs=(whole,) * 4,
        scratch_shapes=[dma((4,))],
        compiler_params=pltpu.CompilerParams(vmem_limit_bytes=1024 * 1024),
    )(o1, n1, o2, n2)
    return (o1.T[None], n1.T[None], o2.T[None], n2.T[None])


def solution(mesh):
    return jax.shard_map(
        on_device,
        mesh=mesh,
        in_specs=(
            P("row", "col", None, "tp"),
            P("row", "col", None, "tp"),
            P("row", "col", None, "tp"),
            P("row", "col", None, None),
            P("row", "col", None),
            P("row", "col"),
            P("col", "tp", "row"),
            P("row", "tp", "col"),
            P("col", "tp", "row"),
            P("row", "tp", "col"),
        ),
        out_specs=(
            P("col", "tp", "row"),
            P("col", "tp", "row"),
            P("row", "tp", "col"),
            P("row", "tp", "col"),
        ),
        check_vma=False,
    )
```

```python
import math

import jax
import jax.numpy as jnp
from jax import lax
from jax.experimental import pallas as pl
from jax.experimental.pallas import tpu as pltpu
from jax.sharding import PartitionSpec as P

D = 2048
H = 8192
TOK = 256
HID = 1024
BLK = 256
SEL = 32
INNER = 4.0
OUTER = 0.7
DECAY = 0.9
MESH = pl.DeviceIdType.MESH
BF = jnp.bfloat16
F32 = jnp.float32

SCALE_MODEL = 1.0 / math.sqrt(D)
SCALE_HIDDEN = 1.0 / math.sqrt(H)
NT = (((1,), (1,)), ((), ()))
HALF = 128


def kernel(
    act_h, res_h, up_h, st_h, ids_h, cnt_v, w1_h, w2_h, m1_h, m2_h,
    o1, n1, o2, n2,
    act, res, up, st, ids, w1g, w2g, m1, m2,
    part, cin, lin, zb, zin, y, relay, pre2, slope, selw, sely, stt, pc1, pc2,
    q, qin, dy, t1, t1in, t2, t2x, t2z, t2zin, wown, wrow, wcol,
    loc, w1s, w1r, w2s, w2r, zs, zr,
    crs, crr, zrs, zrr, ags, agr, cgs, cgr, lrs, lrr, lgs, lgr,
    qs, qr, ds_, dr_, rs_, rr_, xs, xr, as_, ar_, nrs, nrr, ncs, ncr,
):
    r = lax.axis_index("row")
    c = lax.axis_index("col")
    t = lax.axis_index("tp")
    x = lax.div(c, 2)
    zh = lax.rem(c, 2)
    zl = lax.div(t, 2)
    core = lax.rem(t, 2)
    z = zh * 4 + zl
    other = (r, c, zl * 2 + 1 - core)

    def row_dev(d):
        return (lax.rem(r + d, 8), c, t)

    def tp_dev(d):
        return (r, c, lax.rem(t + d, 8))

    def x_dev(d):
        return (r, lax.rem(x + d, 4) * 2 + zh, t)

    def z_dev(d):
        to = lax.rem(z + d, 8)
        return (r, x * 2 + lax.div(to, 4), lax.rem(to, 4) * 2 + core)

    def zl_dev(d):
        return (r, c, lax.rem(zl + d, 4) * 2 + core)

    def col_dev(d):
        return (r, lax.rem(c + d, 8), t)

    antipode = (r, x * 2 + 1 - zh, t)
    pending = []

    def send(src, dst, s_sem, r_sem, device):
        copy = pltpu.make_async_remote_copy(
            src_ref=src, dst_ref=dst, send_sem=s_sem, recv_sem=r_sem,
            device_id=device, device_id_type=MESH,
        )
        copy.start()
        pending.append(copy)

    def arrive(dst, s_sem, r_sem):
        pltpu.make_async_remote_copy(
            src_ref=dst, dst_ref=dst, send_sem=s_sem, recv_sem=r_sem,
            device_id=other, device_id_type=MESH,
        ).wait_recv()

    barrier = pltpu.get_barrier_semaphore()
    partners = [row_dev(1), row_dev(7), x_dev(1), x_dev(3), z_dev(2), z_dev(6), other]
    partners += [zl_dev(d) for d in range(1, 4)]
    for device in partners:
        pl.semaphore_signal(barrier, inc=1, device_id=device, device_id_type=MESH)
    local = [
        pltpu.make_async_copy(a, b, loc.at[k])
        for k, (a, b) in enumerate(
            (
                (w1_h.at[:, pl.ds(0, HALF)], w1g.at[r, 0]), (w1_h.at[:, pl.ds(HALF, HALF)], w1g.at[r, 1]),
                (w2_h, w2g.at[c]), (act_h, act), (res_h, res),
                (up_h, up), (st_h, st), (ids_h, ids), (m1_h, m1), (m2_h, m2),
            )
        )
    ]
    for copy in local:
        copy.start()

    pl.semaphore_wait(barrier, len(partners))

    def chunk(way, step, j):
        return lax.rem(r + (8 - step if way == 0 else step), 8), (j if way == 0 else 1 - j)

    def w1_send(way, step, j):
        ref = w1g.at[chunk(way, step, j)]
        send(ref, ref, w1s.at[way, step, j], w1r.at[way, step, j], row_dev(1 if way == 0 else 7))

    def ring(k):
        step, j = divmod(k - 1, 2)
        for way in range(2):
            arrive(w1g.at[chunk(way, step + 1, j)], w1s.at[way, step, j], w1r.at[way, step, j])
            if step < 2 or (step == 2 and j == 0):
                w1_send(way, step + 1, j)

    def near_half(at, half):
        return w2g.at[lax.rem(at, 4) * 2 + zh, pl.ds(512 * half, 512)]

    def far_quarter(at, quarter):
        return w2g.at[lax.rem(at, 4) * 2 + 1 - zh, pl.ds(256 * quarter, 256)]

    def near_part(way, e, hops):
        half = (0, 1, 0)[e] if way == 0 else (1, 0, 1)[e]
        steps = hops + (1 if e == 2 else 0)
        return near_half(x + (4 - steps if way == 0 else steps), half)

    def far_part(way, e, hops):
        quarter = (0, 2, 1, 3, 0, 1)[e] if way == 0 else (2, 0, 3, 1, 2, 3)[e]
        steps = hops + (1 if e > 3 else 0)
        return far_quarter(x + (4 - steps if way == 0 else steps), quarter)

    def near_send(way, e):
        ref = near_part(way, e, 0)
        send(ref, ref, w2s.at[way, e], w2r.at[way, e], x_dev(1 if way == 0 else 3))

    def near_wait(way, e):
        arrive(near_part(way, e, 1), w2s.at[way, e], w2r.at[way, e])

    def far_send(way, e):
        ref = far_part(way, e, 0)
        send(ref, ref, w2s.at[way, 3 + e], w2r.at[way, 3 + e], x_dev(1 if way == 0 else 3))

    def far_wait(way, e):
        arrive(far_part(way, e, 1), w2s.at[way, 3 + e], w2r.at[way, 3 + e])

    def z_first(way, e):
        send(
            w2g.at[c, pl.ds(512 * way + 256 * e, 256)], relay.at[way, e],
            zs.at[way, e, 0], zr.at[way, e, 0], z_dev(2 if way == 0 else 6),
        )

    def z_second(way, e):
        arrive(relay.at[way, e], zs.at[way, e, 0], zr.at[way, e, 0])
        hop = 2 if way == 0 else 6
        far = lax.div(lax.rem(z + hop, 8), 4)
        send(
            relay.at[way, e], w2g.at[x * 2 + 1 - far, pl.ds(512 * way + 256 * e, 256)],
            zs.at[way, e, 1], zr.at[way, e, 1], z_dev(hop),
        )

    def z_wait(way, e):
        arrive(far_quarter(x, 2 * way + e), zs.at[way, e, 1], zr.at[way, e, 1])

    local[0].wait()
    local[1].wait()
    for j in range(2):
        for way in range(2):
            w1_send(way, 0, j)
    local[2].wait()
    for e in range(2):
        for way in range(2):
            z_first(way, e)
            near_send(way, e)
    for copy in local[3:]:
        copy.wait()

    weight = cnt_v[...].astype(F32)
    wown[...] = jnp.broadcast_to(weight, (8, 128))

    def send_counts():
        for d in range(1, 8):
            send(wown, wrow.at[d - 1], nrs.at[d - 1], nrr.at[d - 1], row_dev(d))
            send(wown, wcol.at[d - 1], ncs.at[d - 1], ncr.at[d - 1], col_dev(d))

    def group(g):
        step, j = (0, 0) if g == 0 else ((g + 1) // 2, (g - 1) % 2)
        first = chunk(0, step, j)
        second = chunk(1, step, j)
        return first, second

    def partial_sum(g):
        (na, ha), (nb, hb) = group(g)
        rhs = jnp.concatenate([w1g[na, ha], w1g[nb, hb]], axis=1)
        acc = jnp.dot(act[...], rhs, preferred_element_type=F32) * SCALE_HIDDEN
        own = []
        for n, half in ((na, ha), (nb, hb)):
            mine = jnp.where(n == t, 1.0, 0.0).astype(F32)
            own.append(res[:, HALF * half : HALF * half + HALF].astype(F32) * mine)
        acc = acc + jnp.concatenate(own, axis=1)
        part[g] = acc.astype(BF).reshape(2, 4, SEL, BLK)

    def stage0(g):
        partial_sum(g)
        send(part.at[g, 1 - core], cin.at[g], crs.at[g], crr.at[g], other)

    def stage1(i):
        arrive(cin.at[i], crs.at[i], crr.at[i])
        both = part[i, core].astype(F32) + cin[i].astype(F32)
        zb[i] = both.astype(BF)
        for d in range(1, 4):
            send(
                zb.at[i, lax.rem(zl + d, 4)], zin.at[i, d - 1],
                zrs.at[i, d - 1], zrr.at[i, d - 1], zl_dev(d),
            )

    def stage2(i):
        total = zb[i, zl].astype(F32)
        for d in range(1, 4):
            arrive(zin.at[i, d - 1], zrs.at[i, d - 1], zrr.at[i, d - 1])
            total = total + zin[i, d - 1].astype(F32)
        y[i, core, zl] = total.astype(BF)
        for d in range(1, 4):
            ref = y.at[i, core, zl]
            send(ref, ref, ags.at[i, d - 1], agr.at[i, d - 1], zl_dev(d))

    def stage3(i):
        for d in range(1, 4):
            arrive(y.at[i, core, lax.rem(zl + 4 - d, 4)], ags.at[i, d - 1], agr.at[i, d - 1])
        ref = y.at[i, core]
        send(ref, ref, cgs.at[i], cgr.at[i], other)

    def stage4(i):
        arrive(y.at[i, 1 - core], cgs.at[i], cgr.at[i])

    def place(d):
        at = lax.rem(t + d, 8)
        return lax.rem(at, 2), lax.div(at, 2)

    def last_out():
        partial_sum(7)
        for d in range(1, 8):
            send(part.at[(7, *place(d))], lin.at[d - 1], lrs.at[d - 1], lrr.at[d - 1], tp_dev(d))

    def last_back():
        total = part[7, core, zl].astype(F32)
        for d in range(1, 8):
            arrive(lin.at[d - 1], lrs.at[d - 1], lrr.at[d - 1])
            total = total + lin[d - 1].astype(F32)
        y[7, core, zl] = total.astype(BF)
        for d in range(1, 8):
            ref = y.at[7, core, zl]
            send(ref, ref, lgs.at[d - 1], lgr.at[d - 1], tp_dev(d))

    def last_wait():
        for d in range(1, 8):
            arrive(y.at[(7, *place(8 - d))], lgs.at[d - 1], lgr.at[d - 1])

    def rows_at(start):
        return (
            lax.broadcasted_iota(jnp.int32, (SEL, BLK), 0) + start
            == lax.broadcasted_iota(jnp.int32, (SEL, BLK), 1)
        ).astype(F32).astype(BF)

    first_rows = rows_at(0)
    other_rows = rows_at(HALF)

    def y_group(g):
        return y[g].reshape(TOK, BLK)

    def back(step):
        return lax.rem(r + 8 - step, 8)

    def ahead(step):
        return lax.rem(r + step, 8)

    def pick_y(n, g, rows):
        sely[n] = lax.dot_general(rows, y_group(g), NT, preferred_element_type=F32).astype(BF)

    def pick_pair(step):
        pick_y(back(step), 2 * step - 1, first_rows)
        pick_y(ahead(step), 2 * step, other_rows)

    def pick_w(n):
        selw[n] = lax.dot_general(first_rows, w2g[n], NT, preferred_element_type=F32).astype(BF)

    def product(values, n):
        return lax.dot_general(values, w2g[n], NT, preferred_element_type=F32)

    def pair(step):
        low, high = y_group(2 * step - 1), y_group(2 * step)
        behind = jnp.concatenate([low[:, :HALF], high[:, :HALF]], axis=1)
        before = jnp.concatenate([high[:, HALF:], low[:, HALF:]], axis=1)
        return product(behind, back(step)) + product(before, ahead(step))

    def prepare():
        keep_row = (ids[...] != 0).astype(F32)
        across = lax.broadcasted_iota(jnp.int32, (TOK, TOK), 0)
        along = lax.broadcasted_iota(jnp.int32, (TOK, TOK), 1)
        keep_col = jnp.sum(
            jnp.where(across == along, jnp.broadcast_to(keep_row, (TOK, TOK)), 0.0),
            axis=1, keepdims=True,
        )
        up[...] = (up[...].astype(F32) * keep_col).astype(BF)
        stt[...] = lax.dot_general(rows_at(SEL * t), st[...], NT, preferred_element_type=F32) * keep_row
        pc1[...] = lax.dot_general(first_rows[:, :HALF], w1g[r, 0], NT, preferred_element_type=F32)
        pc2[...] = lax.dot_general(first_rows, w2g[c], NT, preferred_element_type=F32)

    stage0(0)
    prepare()

    ring(1)
    for way in range(2):
        z_second(way, 0)
    for way in range(2):
        near_wait(way, 0)
        near_send(way, 2)
    stage0(1)

    ring(2)
    stage0(2)
    for way in range(2):
        z_second(way, 1)
    stage1(0)
    for way in range(2):
        near_wait(way, 1)

    ring(3)
    stage0(3)
    stage1(1)
    stage1(2)
    for way in range(2):
        near_wait(way, 2)
    for k in range(4):
        pick_w(2 * k + zh)

    ring(4)
    stage0(4)
    stage2(0)
    stage1(3)
    for way in range(2):
        z_wait(way, 0)
    for e in range(2):
        for way in range(2):
            far_send(way, e)
    stage2(1)
    stage1(4)

    ring(5)
    stage0(5)
    stage2(2)
    for way in range(2):
        z_wait(way, 1)
    for e in range(2, 4):
        for way in range(2):
            far_send(way, e)
    stage3(0)
    stage2(3)
    stage1(5)
    stage3(1)
    stage4(0)
    pick_y(r, 0, first_rows)

    ring(6)
    for way in range(2):
        far_wait(way, 0)
        far_send(way, 4)
    stage0(6)
    stage1(6)
    stage2(4)
    stage3(2)
    stage4(1)
    stage2(5)
    stage4(2)
    pick_pair(1)

    ring(7)
    last_out()
    for way in range(2):
        far_wait(way, 2)
        far_send(way, 5)
    stage2(6)
    stage3(3)
    stage3(4)
    stage4(3)
    stage4(4)
    stage3(5)
    last_back()
    stage3(6)
    for way in range(2):
        for e in (1, 3, 4, 5):
            far_wait(way, e)
    for k in range(4):
        pick_w(2 * k + 1 - zh)
    pre2[...] = product(y_group(0), r) + pair(1)
    pre2[...] += pair(2)
    stage4(5)
    stage4(6)
    pre2[...] += pair(3)
    last_wait()

    last = ahead(4)
    y_last = y_group(7)
    carried = jnp.zeros((BLK, TOK), F32)
    for k in range(4):
        cols = slice(256 * k, 256 * k + 256)
        pre = pre2[:, cols] + lax.dot_general(
            y_last, w2g[last, cols], NT, preferred_element_type=F32
        )
        pre = pre * SCALE_MODEL
        squash = jax.nn.sigmoid(pre)
        piece = (up[:, cols].astype(F32) * squash * (1.0 + pre * (1.0 - squash))).astype(BF)
        slope[:, cols] = piece
        carried = carried + lax.dot_general(
            selw[:, :, cols].reshape(BLK, 256), piece, NT, preferred_element_type=F32
        )
    q[...] = (carried * SCALE_MODEL).astype(BF).reshape(8, SEL, TOK)
    for d in range(1, 8):
        send(q.at[lax.rem(t + d, 8)], qin.at[d - 1], qs.at[d - 1], qr.at[d - 1], tp_dev(d))

    pick_pair(2)
    pick_pair(3)
    pick_y(last, 7, first_rows)
    factor = weight * INNER
    grad = jnp.dot(sely[...].reshape(BLK, TOK), slope[...], preferred_element_type=F32) * SCALE_MODEL
    t2[...] = (factor * grad).astype(BF).reshape(4, 2, SEL, HID)
    for d in range(1, 4):
        send(t2.at[lax.rem(x + d, 4)], t2x.at[d - 1], xs.at[d - 1], xr.at[d - 1], x_dev(d))

    total = q[t].astype(F32) + stt[...]
    for d in range(1, 8):
        arrive(qin.at[d - 1], qs.at[d - 1], qr.at[d - 1])
        total = total + qin[d - 1].astype(F32)
    dy[t] = total.astype(BF)
    for d in range(1, 8):
        ref = dy.at[t]
        send(ref, ref, ds_.at[d - 1], dr_.at[d - 1], tp_dev(d))
    send_counts()
    for d in range(1, 8):
        arrive(dy.at[lax.rem(t + 8 - d, 8)], ds_.at[d - 1], dr_.at[d - 1])
    grad = jnp.dot(dy[...].reshape(BLK, TOK), act[...], preferred_element_type=F32) * SCALE_HIDDEN
    t1[...] = (factor * grad).astype(BF).reshape(8, SEL, HID)

    def row_send(d):
        send(t1.at[lax.rem(r + d, 8)], t1in.at[d - 1], rs_.at[d - 1], rr_.at[d - 1], row_dev(d))

    before_rows = len(pending)
    joint = jnp.where(core == 0, 5, 3)
    send(t1.at[lax.rem(r + 4, 8)], t1in.at[3], rs_.at[3], rr_.at[3], row_dev(jnp.where(core == 0, 7, 1)))
    row_send(8 - joint)
    row_send(2)
    row_send(6)

    far = t2[x, 1 - zh].astype(F32)
    near = t2[x, zh].astype(F32)
    for d in range(1, 4):
        arrive(t2x.at[d - 1], xs.at[d - 1], xr.at[d - 1])
        far = far + t2x[d - 1, 1 - zh].astype(F32)
        near = near + t2x[d - 1, zh].astype(F32)
    t2z[...] = far.astype(BF)
    send(t2z, t2zin, as_, ar_, antipode)

    arrive(t1in.at[3], rs_.at[3], rr_.at[3])
    to = lax.rem(r + joint, 8)
    t1[to] = (t1[to].astype(F32) + t1in[3].astype(F32)).astype(BF)
    row_send(joint)
    row_send(1)
    row_send(7)

    def total_of(buffer, s_sems, r_sems):
        count = wown[...]
        for d in range(1, 8):
            arrive(buffer.at[d - 1], s_sems.at[d - 1], r_sems.at[d - 1])
            count = count + buffer[d - 1]
        return count[0:1, 0:1]

    total_one = total_of(wrow, nrs, nrr)
    total_two = total_of(wcol, ncs, ncr)

    arrive(t2zin, as_, ar_)
    delta = (near + t2zin[...].astype(F32)) / total_two
    moment = DECAY * m2[...] + delta
    n2[...] = moment
    o2[...] = pc2[...] - OUTER * (delta + DECAY * moment)

    for copy in pending[:before_rows]:
        copy.wait_send()
    summed = t1[r].astype(F32)
    for d in (2, 6, 3, 5, 1, 7):
        arrive(t1in.at[d - 1], rs_.at[d - 1], rr_.at[d - 1])
        summed = summed + t1in[d - 1].astype(F32)
    delta = summed / total_one
    moment = DECAY * m1[...] + delta
    n1[...] = moment
    o1[...] = pc1[...] - OUTER * (delta + DECAY * moment)

    for copy in pending[before_rows:]:
        copy.wait_send()


def write_out(a, b, c, d, a_out, b_out, c_out, d_out, sems):
    copies = [
        pltpu.make_async_copy(src, dst, sems.at[k])
        for k, (src, dst) in enumerate(((a, a_out), (b, b_out), (c, c_out), (d, d_out)))
    ]
    for copy in copies:
        copy.start()
    for copy in copies:
        copy.wait()


def in_hbm(value):
    return pltpu.with_memory_space_constraint(value, pltpu.HBM)


def on_device(
    act_one, residual, upstream, stream_grad, token_ids, shard_counts,
    out_one, in_two, out_one_moment, in_two_moment,
):
    dma = pltpu.SemaphoreType.DMA
    vmem = pltpu.VMEM
    whole = pl.BlockSpec(memory_space=pltpu.HBM)
    inside = pl.BlockSpec(memory_space=pltpu.VMEM)
    scratch = [
        vmem((TOK, HID), BF), vmem((TOK, BLK), BF), vmem((TOK, HID), BF), vmem((TOK, BLK), BF),
        vmem((1, TOK), jnp.int32), vmem((8, 2, HID, HALF), BF), vmem((8, HID, BLK), BF),
        vmem((SEL, HID), F32), vmem((SEL, HID), F32),
        vmem((8, 2, 4, SEL, BLK), BF), vmem((7, 4, SEL, BLK), BF), vmem((7, SEL, BLK), BF),
        vmem((7, 4, SEL, BLK), BF), vmem((7, 3, SEL, BLK), BF),
        vmem((8, 2, 4, SEL, BLK), BF), vmem((2, 2, BLK, BLK), BF),
        vmem((TOK, HID), F32), vmem((TOK, HID), BF), vmem((8, SEL, HID), BF),
        vmem((8, SEL, TOK), BF), vmem((SEL, TOK), F32), vmem((SEL, HID), F32), vmem((SEL, HID), F32),
        vmem((8, SEL, TOK), BF), vmem((7, SEL, TOK), BF), vmem((8, SEL, TOK), BF),
        vmem((8, SEL, HID), BF), vmem((7, SEL, HID), BF),
        vmem((4, 2, SEL, HID), BF), vmem((3, 2, SEL, HID), BF),
        vmem((SEL, HID), BF), vmem((SEL, HID), BF),
        vmem((8, 128), F32), vmem((7, 8, 128), F32), vmem((7, 8, 128), F32),
        dma((10,)),
        dma((2, 4, 2)), dma((2, 4, 2)), dma((2, 9)), dma((2, 9)), dma((2, 2, 2)), dma((2, 2, 2)),
        dma((7,)), dma((7,)), dma((7, 3)), dma((7, 3)), dma((7, 3)), dma((7, 3)), dma((7,)), dma((7,)),
        dma((7,)), dma((7,)), dma((7,)), dma((7,)),
        dma((7,)), dma((7,)), dma((7,)), dma((7,)), dma((7,)), dma((7,)),
        dma((3,)), dma((3,)), dma(()), dma(()), dma((7,)), dma((7,)), dma((7,)), dma((7,)),
    ]
    result = jax.ShapeDtypeStruct((SEL, HID), F32)
    o1, n1, o2, n2 = pl.pallas_call(
        kernel,
        out_shape=(result,) * 4,
        in_specs=[whole] * 5 + [inside] + [whole] * 4,
        out_specs=(inside,) * 4,
        scratch_shapes=scratch,
        compiler_params=pltpu.CompilerParams(
            collective_id=0, has_side_effects=True, vmem_limit_bytes=48 * 1024 * 1024
        ),
        cost_estimate=pl.CostEstimate(flops=3_000_000_000, bytes_accessed=4_000_000, transcendentals=300_000),
    )(
        *map(in_hbm, (act_one[0, 0], residual[0, 0], upstream[0, 0], stream_grad[0, 0], token_ids[0])),
        shard_counts,
        *map(in_hbm, (out_one[0], in_two[0], out_one_moment[0].T, in_two_moment[0].T)),
    )
    o1, n1, o2, n2 = pl.pallas_call(
        write_out,
        out_shape=(result,) * 4,
        in_specs=[pl.BlockSpec(memory_space=pl.ANY)] * 4,
        out_specs=(whole,) * 4,
        scratch_shapes=[dma((4,))],
        compiler_params=pltpu.CompilerParams(vmem_limit_bytes=1024 * 1024),
    )(o1, n1, o2, n2)
    return (o1.T[None], n1.T[None], o2.T[None], n2.T[None])


def solution(mesh):
    return jax.shard_map(
        on_device,
        mesh=mesh,
        in_specs=(
            P("row", "col", None, "tp"),
            P("row", "col", None, "tp"),
            P("row", "col", None, "tp"),
            P("row", "col", None, None),
            P("row", "col", None),
            P("row", "col"),
            P("col", "tp", "row"),
            P("row", "tp", "col"),
            P("col", "tp", "row"),
            P("row", "tp", "col"),
        ),
        out_specs=(
            P("col", "tp", "row"),
            P("col", "tp", "row"),
            P("row", "tp", "col"),
            P("row", "tp", "col"),
        ),
        check_vma=False,
    )
```

```python
import math

import jax
import jax.numpy as jnp
from jax import lax
from jax.experimental import pallas as pl
from jax.experimental.pallas import tpu as pltpu
from jax.sharding import PartitionSpec as P

D = 2048
H = 8192
TOK = 256
HID = 1024
BLK = 256
SEL = 32
INNER = 4.0
OUTER = 0.7
DECAY = 0.9
MESH = pl.DeviceIdType.MESH
BF = jnp.bfloat16
F32 = jnp.float32

SCALE_MODEL = 1.0 / math.sqrt(D)
SCALE_HIDDEN = 1.0 / math.sqrt(H)
NT = (((1,), (1,)), ((), ()))
HALF = 128


def kernel(
    act_h, res_h, up_h, st_h, ids_h, cnt_v, w1_h, w2_h, m1_h, m2_h,
    o1, n1, o2, n2,
    act, res, up, st, ids, w1g, w2g, m1, m2,
    part, cin, lin, zb, zin, y, relay, pre2, slope, selw, sely, stt, pc1, pc2,
    q, qin, dy, t1, t1in, t2, t2x, t2z, t2zin, wown, wrow, wcol,
    loc, w1s, w1r, w2s, w2r, zs, zr,
    crs, crr, zrs, zrr, ags, agr, cgs, cgr, lrs, lrr, lgs, lgr,
    qs, qr, ds_, dr_, rs_, rr_, xs, xr, as_, ar_, nrs, nrr, ncs, ncr,
):
    r = lax.axis_index("row")
    c = lax.axis_index("col")
    t = lax.axis_index("tp")
    x = lax.div(c, 2)
    zh = lax.rem(c, 2)
    zl = lax.div(t, 2)
    core = lax.rem(t, 2)
    z = zh * 4 + zl
    other = (r, c, zl * 2 + 1 - core)

    def row_dev(d):
        return (lax.rem(r + d, 8), c, t)

    def x_dev(d):
        return (r, lax.rem(x + d, 4) * 2 + zh, t)

    def z_dev(d):
        to = lax.rem(z + d, 8)
        return (r, x * 2 + lax.div(to, 4), lax.rem(to, 4) * 2 + core)

    def zl_dev(d):
        return (r, c, lax.rem(zl + d, 4) * 2 + core)

    def col_dev(d):
        return (r, lax.rem(c + d, 8), t)

    end = jnp.where((zl == 0) | (zl == 3), 1, 0)
    down = jnp.where(zl < 2, 0, 1)

    def peer(p):
        if p == 6:
            return zl * 2 + 1 - core
        far = (3, 2 * end, 2 - end)[p // 2]
        to = far + down * (3 - 2 * far)
        return to * 2 + (core if p % 2 == 0 else 1 - core)

    antipode = (r, x * 2 + 1 - zh, t)
    pending = []

    def send(src, dst, s_sem, r_sem, device):
        copy = pltpu.make_async_remote_copy(
            src_ref=src, dst_ref=dst, send_sem=s_sem, recv_sem=r_sem,
            device_id=device, device_id_type=MESH,
        )
        copy.start()
        pending.append(copy)

    def arrive(dst, s_sem, r_sem):
        pltpu.make_async_remote_copy(
            src_ref=dst, dst_ref=dst, send_sem=s_sem, recv_sem=r_sem,
            device_id=other, device_id_type=MESH,
        ).wait_recv()

    barrier = pltpu.get_barrier_semaphore()
    partners = [row_dev(1), row_dev(7), x_dev(1), x_dev(3), z_dev(2), z_dev(6), other]
    partners += [zl_dev(d) for d in range(1, 4)]
    for device in partners:
        pl.semaphore_signal(barrier, inc=1, device_id=device, device_id_type=MESH)
    local = [
        pltpu.make_async_copy(a, b, loc.at[k])
        for k, (a, b) in enumerate(
            (
                (w1_h.at[:, pl.ds(0, HALF)], w1g.at[r, 0]), (w1_h.at[:, pl.ds(HALF, HALF)], w1g.at[r, 1]),
                (w2_h, w2g.at[c]), (act_h, act), (res_h, res),
                (up_h, up), (st_h, st), (ids_h, ids), (m1_h, m1), (m2_h, m2),
            )
        )
    ]
    for copy in local:
        copy.start()

    pl.semaphore_wait(barrier, len(partners))

    def chunk(way, step, j):
        return lax.rem(r + (8 - step if way == 0 else step), 8), (j if way == 0 else 1 - j)

    def w1_send(way, step, j):
        ref = w1g.at[chunk(way, step, j)]
        send(ref, ref, w1s.at[way, step, j], w1r.at[way, step, j], row_dev(1 if way == 0 else 7))

    def ring(k):
        step, j = divmod(k - 1, 2)
        for way in range(2):
            arrive(w1g.at[chunk(way, step + 1, j)], w1s.at[way, step, j], w1r.at[way, step, j])
            if step < 2 or (step == 2 and j == 0):
                w1_send(way, step + 1, j)

    def near_half(at, half):
        return w2g.at[lax.rem(at, 4) * 2 + zh, pl.ds(512 * half, 512)]

    def far_quarter(at, quarter):
        return w2g.at[lax.rem(at, 4) * 2 + 1 - zh, pl.ds(256 * quarter, 256)]

    def near_part(way, e, hops):
        half = (0, 1, 0)[e] if way == 0 else (1, 0, 1)[e]
        steps = hops + (1 if e == 2 else 0)
        return near_half(x + (4 - steps if way == 0 else steps), half)

    def far_part(way, e, hops):
        quarter = (0, 2, 1, 3, 0, 1)[e] if way == 0 else (2, 0, 3, 1, 2, 3)[e]
        steps = hops + (1 if e > 3 else 0)
        return far_quarter(x + (4 - steps if way == 0 else steps), quarter)

    def near_send(way, e):
        ref = near_part(way, e, 0)
        send(ref, ref, w2s.at[way, e], w2r.at[way, e], x_dev(1 if way == 0 else 3))

    def near_wait(way, e):
        arrive(near_part(way, e, 1), w2s.at[way, e], w2r.at[way, e])

    def far_send(way, e):
        ref = far_part(way, e, 0)
        send(ref, ref, w2s.at[way, 3 + e], w2r.at[way, 3 + e], x_dev(1 if way == 0 else 3))

    def far_wait(way, e):
        arrive(far_part(way, e, 1), w2s.at[way, 3 + e], w2r.at[way, 3 + e])

    def z_first(way, e):
        send(
            w2g.at[c, pl.ds(512 * way + 256 * e, 256)], relay.at[way, e],
            zs.at[way, e, 0], zr.at[way, e, 0], z_dev(2 if way == 0 else 6),
        )

    def z_second(way, e):
        arrive(relay.at[way, e], zs.at[way, e, 0], zr.at[way, e, 0])
        hop = 2 if way == 0 else 6
        far = lax.div(lax.rem(z + hop, 8), 4)
        send(
            relay.at[way, e], w2g.at[x * 2 + 1 - far, pl.ds(512 * way + 256 * e, 256)],
            zs.at[way, e, 1], zr.at[way, e, 1], z_dev(hop),
        )

    def z_wait(way, e):
        arrive(far_quarter(x, 2 * way + e), zs.at[way, e, 1], zr.at[way, e, 1])

    local[0].wait()
    local[1].wait()
    for j in range(2):
        for way in range(2):
            w1_send(way, 0, j)
    local[2].wait()
    for e in range(2):
        for way in range(2):
            z_first(way, e)
            near_send(way, e)
    for copy in local[3:]:
        copy.wait()

    weight = cnt_v[...].astype(F32)
    wown[...] = jnp.broadcast_to(weight, (8, 128))

    def send_counts():
        for d in range(1, 8):
            send(wown, wrow.at[d - 1], nrs.at[d - 1], nrr.at[d - 1], row_dev(d))
            send(wown, wcol.at[d - 1], ncs.at[d - 1], ncr.at[d - 1], col_dev(d))

    def group(g):
        step, j = (0, 0) if g == 0 else ((g + 1) // 2, (g - 1) % 2)
        first = chunk(0, step, j)
        second = chunk(1, step, j)
        return first, second

    def partial_sum(g):
        (na, ha), (nb, hb) = group(g)
        rhs = jnp.concatenate([w1g[na, ha], w1g[nb, hb]], axis=1)
        acc = jnp.dot(act[...], rhs, preferred_element_type=F32) * SCALE_HIDDEN
        own = []
        for n, half in ((na, ha), (nb, hb)):
            mine = jnp.where(n == t, 1.0, 0.0).astype(F32)
            own.append(res[:, HALF * half : HALF * half + HALF].astype(F32) * mine)
        acc = acc + jnp.concatenate(own, axis=1)
        part[g] = acc.astype(BF).reshape(2, 4, SEL, BLK)

    def stage0(g):
        partial_sum(g)
        send(part.at[g, 1 - core], cin.at[g], crs.at[g], crr.at[g], other)

    def stage1(i):
        arrive(cin.at[i], crs.at[i], crr.at[i])
        both = part[i, core].astype(F32) + cin[i].astype(F32)
        zb[i] = both.astype(BF)
        for d in range(1, 4):
            send(
                zb.at[i, lax.rem(zl + d, 4)], zin.at[i, d - 1],
                zrs.at[i, d - 1], zrr.at[i, d - 1], zl_dev(d),
            )

    def stage2(i):
        total = zb[i, zl].astype(F32)
        for d in range(1, 4):
            arrive(zin.at[i, d - 1], zrs.at[i, d - 1], zrr.at[i, d - 1])
            total = total + zin[i, d - 1].astype(F32)
        y[i, core, zl] = total.astype(BF)
        for d in range(1, 4):
            ref = y.at[i, core, zl]
            send(ref, ref, ags.at[i, d - 1], agr.at[i, d - 1], zl_dev(d))

    def stage3(i):
        for d in range(1, 4):
            arrive(y.at[i, core, lax.rem(zl + 4 - d, 4)], ags.at[i, d - 1], agr.at[i, d - 1])
        ref = y.at[i, core]
        send(ref, ref, cgs.at[i], cgr.at[i], other)

    def stage4(i):
        arrive(y.at[i, 1 - core], cgs.at[i], cgr.at[i])

    def place(at):
        return lax.rem(at, 2), lax.div(at, 2)

    def last_out():
        partial_sum(7)
        for p in range(7):
            to = peer(p)
            send(part.at[(7, *place(to))], lin.at[t], lrs.at[to], lrr.at[t], (r, c, to))

    def last_back():
        total = part[7, core, zl].astype(F32)
        for p in range(6, -1, -1):
            by = peer(p)
            arrive(lin.at[by], lrs.at[by], lrr.at[by])
            total = total + lin[by].astype(F32)
        y[7, core, zl] = total.astype(BF)
        for p in range(7):
            to = peer(p)
            ref = y.at[7, core, zl]
            send(ref, ref, lgs.at[to], lgr.at[t], (r, c, to))

    def last_wait():
        for p in range(6, -1, -1):
            by = peer(p)
            arrive(y.at[(7, *place(by))], lgs.at[by], lgr.at[by])

    def rows_at(start):
        return (
            lax.broadcasted_iota(jnp.int32, (SEL, BLK), 0) + start
            == lax.broadcasted_iota(jnp.int32, (SEL, BLK), 1)
        ).astype(F32).astype(BF)

    first_rows = rows_at(0)
    other_rows = rows_at(HALF)

    def y_group(g):
        return y[g].reshape(TOK, BLK)

    def back(step):
        return lax.rem(r + 8 - step, 8)

    def ahead(step):
        return lax.rem(r + step, 8)

    def pick_y(n, g, rows):
        sely[n] = lax.dot_general(rows, y_group(g), NT, preferred_element_type=F32).astype(BF)

    def pick_pair(step):
        pick_y(back(step), 2 * step - 1, first_rows)
        pick_y(ahead(step), 2 * step, other_rows)

    def pick_w(n):
        selw[n] = lax.dot_general(first_rows, w2g[n], NT, preferred_element_type=F32).astype(BF)

    def product(values, n):
        return lax.dot_general(values, w2g[n], NT, preferred_element_type=F32)

    def pair(step):
        low, high = y_group(2 * step - 1), y_group(2 * step)
        behind = jnp.concatenate([low[:, :HALF], high[:, :HALF]], axis=1)
        before = jnp.concatenate([high[:, HALF:], low[:, HALF:]], axis=1)
        return product(behind, back(step)) + product(before, ahead(step))

    def prepare():
        keep_row = (ids[...] != 0).astype(F32)
        across = lax.broadcasted_iota(jnp.int32, (TOK, TOK), 0)
        along = lax.broadcasted_iota(jnp.int32, (TOK, TOK), 1)
        keep_col = jnp.sum(
            jnp.where(across == along, jnp.broadcast_to(keep_row, (TOK, TOK)), 0.0),
            axis=1, keepdims=True,
        )
        up[...] = (up[...].astype(F32) * keep_col).astype(BF)
        stt[...] = lax.dot_general(rows_at(SEL * t), st[...], NT, preferred_element_type=F32) * keep_row
        pc1[...] = lax.dot_general(first_rows[:, :HALF], w1g[r, 0], NT, preferred_element_type=F32)
        pc2[...] = lax.dot_general(first_rows, w2g[c], NT, preferred_element_type=F32)

    stage0(0)
    prepare()

    ring(1)
    for way in range(2):
        z_second(way, 0)
    for way in range(2):
        near_wait(way, 0)
        near_send(way, 2)
    stage0(1)

    ring(2)
    stage0(2)
    for way in range(2):
        z_second(way, 1)
    stage1(0)
    for way in range(2):
        near_wait(way, 1)

    ring(3)
    stage0(3)
    stage1(1)
    stage1(2)
    for way in range(2):
        near_wait(way, 2)
    for k in range(4):
        pick_w(2 * k + zh)

    ring(4)
    stage0(4)
    stage2(0)
    stage1(3)
    for way in range(2):
        z_wait(way, 0)
    for e in range(2):
        for way in range(2):
            far_send(way, e)
    stage2(1)
    stage1(4)

    ring(5)
    stage0(5)
    stage2(2)
    for way in range(2):
        z_wait(way, 1)
    for e in range(2, 4):
        for way in range(2):
            far_send(way, e)
    stage3(0)
    stage2(3)
    stage1(5)
    stage3(1)
    stage4(0)
    pick_y(r, 0, first_rows)

    ring(6)
    for way in range(2):
        far_wait(way, 0)
        far_send(way, 4)
    stage0(6)
    stage1(6)
    stage2(4)
    stage3(2)
    stage4(1)
    stage2(5)
    stage4(2)
    pick_pair(1)

    ring(7)
    last_out()
    for way in range(2):
        far_wait(way, 2)
        far_send(way, 5)
    stage2(6)
    stage3(3)
    stage3(4)
    stage4(3)
    stage4(4)
    stage3(5)
    last_back()
    stage3(6)
    for way in range(2):
        for e in (1, 3, 4, 5):
            far_wait(way, e)
    for k in range(4):
        pick_w(2 * k + 1 - zh)
    pre2[...] = product(y_group(0), r) + pair(1)
    pre2[...] += pair(2)
    stage4(5)
    stage4(6)
    pre2[...] += pair(3)
    last_wait()

    last = ahead(4)
    y_last = y_group(7)
    carried = jnp.zeros((BLK, TOK), F32)
    for k in range(4):
        cols = slice(256 * k, 256 * k + 256)
        pre = pre2[:, cols] + lax.dot_general(
            y_last, w2g[last, cols], NT, preferred_element_type=F32
        )
        pre = pre * SCALE_MODEL
        squash = jax.nn.sigmoid(pre)
        piece = (up[:, cols].astype(F32) * squash * (1.0 + pre * (1.0 - squash))).astype(BF)
        slope[:, cols] = piece
        carried = carried + lax.dot_general(
            selw[:, :, cols].reshape(BLK, 256), piece, NT, preferred_element_type=F32
        )
    q[...] = (carried * SCALE_MODEL).astype(BF).reshape(8, SEL, TOK)
    for p in range(7):
        to = peer(p)
        send(q.at[to], qin.at[t], qs.at[to], qr.at[t], (r, c, to))

    pick_pair(2)
    pick_pair(3)
    pick_y(last, 7, first_rows)
    factor = weight * INNER
    grad = jnp.dot(sely[...].reshape(BLK, TOK), slope[...], preferred_element_type=F32) * SCALE_MODEL
    t2[...] = (factor * grad).astype(BF).reshape(4, 2, SEL, HID)
    for d in range(1, 4):
        send(t2.at[lax.rem(x + d, 4)], t2x.at[d - 1], xs.at[d - 1], xr.at[d - 1], x_dev(d))

    total = q[t].astype(F32) + stt[...]
    for p in range(6, -1, -1):
        by = peer(p)
        arrive(qin.at[by], qs.at[by], qr.at[by])
        total = total + qin[by].astype(F32)
    dy[t] = total.astype(BF)
    for p in range(7):
        to = peer(p)
        ref = dy.at[t]
        send(ref, ref, ds_.at[to], dr_.at[t], (r, c, to))
    send_counts()
    for p in range(6, -1, -1):
        by = peer(p)
        arrive(dy.at[by], ds_.at[by], dr_.at[by])
    grad = jnp.dot(dy[...].reshape(BLK, TOK), act[...], preferred_element_type=F32) * SCALE_HIDDEN
    t1[...] = (factor * grad).astype(BF).reshape(8, SEL, HID)

    def row_send(d):
        send(t1.at[lax.rem(r + d, 8)], t1in.at[d - 1], rs_.at[d - 1], rr_.at[d - 1], row_dev(d))

    before_rows = len(pending)
    joint = jnp.where(core == 0, 5, 3)
    send(t1.at[lax.rem(r + 4, 8)], t1in.at[3], rs_.at[3], rr_.at[3], row_dev(jnp.where(core == 0, 7, 1)))
    row_send(8 - joint)
    row_send(2)
    row_send(6)

    far = t2[x, 1 - zh].astype(F32)
    near = t2[x, zh].astype(F32)
    for d in range(1, 4):
        arrive(t2x.at[d - 1], xs.at[d - 1], xr.at[d - 1])
        far = far + t2x[d - 1, 1 - zh].astype(F32)
        near = near + t2x[d - 1, zh].astype(F32)
    t2z[...] = far.astype(BF)
    send(t2z, t2zin, as_, ar_, antipode)

    arrive(t1in.at[3], rs_.at[3], rr_.at[3])
    to = lax.rem(r + joint, 8)
    t1[to] = (t1[to].astype(F32) + t1in[3].astype(F32)).astype(BF)
    row_send(joint)
    row_send(1)
    row_send(7)

    def total_of(buffer, s_sems, r_sems):
        count = wown[...]
        for d in range(1, 8):
            arrive(buffer.at[d - 1], s_sems.at[d - 1], r_sems.at[d - 1])
            count = count + buffer[d - 1]
        return count[0:1, 0:1]

    total_one = total_of(wrow, nrs, nrr)
    total_two = total_of(wcol, ncs, ncr)

    arrive(t2zin, as_, ar_)
    delta = (near + t2zin[...].astype(F32)) / total_two
    moment = DECAY * m2[...] + delta
    n2[...] = moment
    o2[...] = pc2[...] - OUTER * (delta + DECAY * moment)

    for copy in pending[:before_rows]:
        copy.wait_send()
    summed = t1[r].astype(F32)
    for d in (2, 6, 3, 5, 1, 7):
        arrive(t1in.at[d - 1], rs_.at[d - 1], rr_.at[d - 1])
        summed = summed + t1in[d - 1].astype(F32)
    delta = summed / total_one
    moment = DECAY * m1[...] + delta
    n1[...] = moment
    o1[...] = pc1[...] - OUTER * (delta + DECAY * moment)

    for copy in pending[before_rows:]:
        copy.wait_send()


def write_out(a, b, c, d, a_out, b_out, c_out, d_out, sems):
    copies = [
        pltpu.make_async_copy(src, dst, sems.at[k])
        for k, (src, dst) in enumerate(((a, a_out), (b, b_out), (c, c_out), (d, d_out)))
    ]
    for copy in copies:
        copy.start()
    for copy in copies:
        copy.wait()


def in_hbm(value):
    return pltpu.with_memory_space_constraint(value, pltpu.HBM)


def on_device(
    act_one, residual, upstream, stream_grad, token_ids, shard_counts,
    out_one, in_two, out_one_moment, in_two_moment,
):
    dma = pltpu.SemaphoreType.DMA
    vmem = pltpu.VMEM
    whole = pl.BlockSpec(memory_space=pltpu.HBM)
    inside = pl.BlockSpec(memory_space=pltpu.VMEM)
    scratch = [
        vmem((TOK, HID), BF), vmem((TOK, BLK), BF), vmem((TOK, HID), BF), vmem((TOK, BLK), BF),
        vmem((1, TOK), jnp.int32), vmem((8, 2, HID, HALF), BF), vmem((8, HID, BLK), BF),
        vmem((SEL, HID), F32), vmem((SEL, HID), F32),
        vmem((8, 2, 4, SEL, BLK), BF), vmem((7, 4, SEL, BLK), BF), vmem((8, SEL, BLK), BF),
        vmem((7, 4, SEL, BLK), BF), vmem((7, 3, SEL, BLK), BF),
        vmem((8, 2, 4, SEL, BLK), BF), vmem((2, 2, BLK, BLK), BF),
        vmem((TOK, HID), F32), vmem((TOK, HID), BF), vmem((8, SEL, HID), BF),
        vmem((8, SEL, TOK), BF), vmem((SEL, TOK), F32), vmem((SEL, HID), F32), vmem((SEL, HID), F32),
        vmem((8, SEL, TOK), BF), vmem((8, SEL, TOK), BF), vmem((8, SEL, TOK), BF),
        vmem((8, SEL, HID), BF), vmem((7, SEL, HID), BF),
        vmem((4, 2, SEL, HID), BF), vmem((3, 2, SEL, HID), BF),
        vmem((SEL, HID), BF), vmem((SEL, HID), BF),
        vmem((8, 128), F32), vmem((7, 8, 128), F32), vmem((7, 8, 128), F32),
        dma((10,)),
        dma((2, 4, 2)), dma((2, 4, 2)), dma((2, 9)), dma((2, 9)), dma((2, 2, 2)), dma((2, 2, 2)),
        dma((7,)), dma((7,)), dma((7, 3)), dma((7, 3)), dma((7, 3)), dma((7, 3)), dma((7,)), dma((7,)),
        dma((8,)), dma((8,)), dma((8,)), dma((8,)),
        dma((8,)), dma((8,)), dma((8,)), dma((8,)), dma((7,)), dma((7,)),
        dma((3,)), dma((3,)), dma(()), dma(()), dma((7,)), dma((7,)), dma((7,)), dma((7,)),
    ]
    result = jax.ShapeDtypeStruct((SEL, HID), F32)
    o1, n1, o2, n2 = pl.pallas_call(
        kernel,
        out_shape=(result,) * 4,
        in_specs=[whole] * 5 + [inside] + [whole] * 4,
        out_specs=(inside,) * 4,
        scratch_shapes=scratch,
        compiler_params=pltpu.CompilerParams(
            collective_id=0, has_side_effects=True, vmem_limit_bytes=48 * 1024 * 1024
        ),
        cost_estimate=pl.CostEstimate(flops=3_000_000_000, bytes_accessed=4_000_000, transcendentals=300_000),
    )(
        *map(in_hbm, (act_one[0, 0], residual[0, 0], upstream[0, 0], stream_grad[0, 0], token_ids[0])),
        shard_counts,
        *map(in_hbm, (out_one[0], in_two[0], out_one_moment[0].T, in_two_moment[0].T)),
    )
    o1, n1, o2, n2 = pl.pallas_call(
        write_out,
        out_shape=(result,) * 4,
        in_specs=[pl.BlockSpec(memory_space=pl.ANY)] * 4,
        out_specs=(whole,) * 4,
        scratch_shapes=[dma((4,))],
        compiler_params=pltpu.CompilerParams(vmem_limit_bytes=1024 * 1024),
    )(o1, n1, o2, n2)
    return (o1.T[None], n1.T[None], o2.T[None], n2.T[None])


def solution(mesh):
    return jax.shard_map(
        on_device,
        mesh=mesh,
        in_specs=(
            P("row", "col", None, "tp"),
            P("row", "col", None, "tp"),
            P("row", "col", None, "tp"),
            P("row", "col", None, None),
            P("row", "col", None),
            P("row", "col"),
            P("col", "tp", "row"),
            P("row", "tp", "col"),
            P("col", "tp", "row"),
            P("row", "tp", "col"),
        ),
        out_specs=(
            P("col", "tp", "row"),
            P("col", "tp", "row"),
            P("row", "tp", "col"),
            P("row", "tp", "col"),
        ),
        check_vma=False,
    )
```

```python
import math

import jax
import jax.numpy as jnp
from jax import lax
from jax.experimental import pallas as pl
from jax.experimental.pallas import tpu as pltpu
from jax.sharding import PartitionSpec as P

D = 2048
H = 8192
TOK = 256
HID = 1024
BLK = 256
SEL = 32
INNER = 4.0
OUTER = 0.7
DECAY = 0.9
MESH = pl.DeviceIdType.MESH
BF = jnp.bfloat16
F32 = jnp.float32

SCALE_MODEL = 1.0 / math.sqrt(D)
SCALE_HIDDEN = 1.0 / math.sqrt(H)
NT = (((1,), (1,)), ((), ()))
HALF = 128


def kernel(
    act_h, res_h, up_h, st_h, ids_h, cnt_v, w1_h, w2_h, m1_h, m2_h,
    o1, n1, o2, n2,
    act, res, up, st, ids, w1g, w2g, m1, m2,
    part, cin, lin, zb, zin, y, relay, pre2, slope, selw, sely, stt, pc1, pc2,
    q, qin, dy, t1, t1in, t2, t2x, t2z, t2zin, wown, wrow, wcol,
    loc, w1s, w1r, w2s, w2r, zs, zr,
    crs, crr, zrs, zrr, ags, agr, cgs, cgr, lrs, lrr, lgs, lgr,
    qs, qr, ds_, dr_, rs_, rr_, xs, xr, as_, ar_, nrs, nrr, ncs, ncr,
):
    r = lax.axis_index("row")
    c = lax.axis_index("col")
    t = lax.axis_index("tp")
    x = lax.div(c, 2)
    zh = lax.rem(c, 2)
    zl = lax.div(t, 2)
    core = lax.rem(t, 2)
    z = zh * 4 + zl
    other = (r, c, zl * 2 + 1 - core)

    def row_dev(d):
        return (lax.rem(r + d, 8), c, t)

    def tp_dev(d):
        return (r, c, lax.rem(t + d, 8))

    def x_dev(d):
        return (r, lax.rem(x + d, 4) * 2 + zh, t)

    def z_dev(d):
        to = lax.rem(z + d, 8)
        return (r, x * 2 + lax.div(to, 4), lax.rem(to, 4) * 2 + core)

    def zl_dev(d):
        return (r, c, lax.rem(zl + d, 4) * 2 + core)

    def col_dev(d):
        return (r, lax.rem(c + d, 8), t)

    antipode = (r, x * 2 + 1 - zh, t)
    pending = []

    def send(src, dst, s_sem, r_sem, device):
        copy = pltpu.make_async_remote_copy(
            src_ref=src, dst_ref=dst, send_sem=s_sem, recv_sem=r_sem,
            device_id=device, device_id_type=MESH,
        )
        copy.start()
        pending.append(copy)

    def arrive(dst, s_sem, r_sem):
        pltpu.make_async_remote_copy(
            src_ref=dst, dst_ref=dst, send_sem=s_sem, recv_sem=r_sem,
            device_id=other, device_id_type=MESH,
        ).wait_recv()

    barrier = pltpu.get_barrier_semaphore()
    partners = [row_dev(1), row_dev(7), x_dev(1), x_dev(3), z_dev(2), z_dev(6), other]
    partners += [zl_dev(d) for d in range(1, 4)]
    for device in partners:
        pl.semaphore_signal(barrier, inc=1, device_id=device, device_id_type=MESH)
    local = [
        pltpu.make_async_copy(a, b, loc.at[k])
        for k, (a, b) in enumerate(
            (
                (w1_h.at[:, pl.ds(0, HALF)], w1g.at[r, 0]), (w1_h.at[:, pl.ds(HALF, HALF)], w1g.at[r, 1]),
                (w2_h, w2g.at[c]), (act_h, act), (res_h, res),
                (up_h, up), (st_h, st), (ids_h, ids), (m1_h, m1), (m2_h, m2),
            )
        )
    ]
    for copy in local:
        copy.start()

    pl.semaphore_wait(barrier, len(partners))

    def chunk(way, step, j):
        return lax.rem(r + (8 - step if way == 0 else step), 8), (j if way == 0 else 1 - j)

    def w1_send(way, step, j):
        ref = w1g.at[chunk(way, step, j)]
        send(ref, ref, w1s.at[way, step, j], w1r.at[way, step, j], row_dev(1 if way == 0 else 7))

    def ring(k):
        step, j = divmod(k - 1, 2)
        for way in range(2):
            arrive(w1g.at[chunk(way, step + 1, j)], w1s.at[way, step, j], w1r.at[way, step, j])
            if step < 2 or (step == 2 and j == 0):
                w1_send(way, step + 1, j)

    def near_half(at, half):
        return w2g.at[lax.rem(at, 4) * 2 + zh, pl.ds(512 * half, 512)]

    def far_quarter(at, quarter):
        return w2g.at[lax.rem(at, 4) * 2 + 1 - zh, pl.ds(256 * quarter, 256)]

    def near_part(way, e, hops):
        half = (0, 1, 0)[e] if way == 0 else (1, 0, 1)[e]
        steps = hops + (1 if e == 2 else 0)
        return near_half(x + (4 - steps if way == 0 else steps), half)

    def far_part(way, e, hops):
        quarter = (0, 2, 1, 3, 0, 1)[e] if way == 0 else (2, 0, 3, 1, 2, 3)[e]
        steps = hops + (1 if e > 3 else 0)
        return far_quarter(x + (4 - steps if way == 0 else steps), quarter)

    def near_send(way, e):
        ref = near_part(way, e, 0)
        send(ref, ref, w2s.at[way, e], w2r.at[way, e], x_dev(1 if way == 0 else 3))

    def near_wait(way, e):
        arrive(near_part(way, e, 1), w2s.at[way, e], w2r.at[way, e])

    def far_send(way, e):
        ref = far_part(way, e, 0)
        send(ref, ref, w2s.at[way, 3 + e], w2r.at[way, 3 + e], x_dev(1 if way == 0 else 3))

    def far_wait(way, e):
        arrive(far_part(way, e, 1), w2s.at[way, 3 + e], w2r.at[way, 3 + e])

    def z_first(way, e):
        send(
            w2g.at[c, pl.ds(512 * way + 256 * e, 256)], relay.at[way, e],
            zs.at[way, e, 0], zr.at[way, e, 0], z_dev(2 if way == 0 else 6),
        )

    def z_second(way, e):
        arrive(relay.at[way, e], zs.at[way, e, 0], zr.at[way, e, 0])
        hop = 2 if way == 0 else 6
        far = lax.div(lax.rem(z + hop, 8), 4)
        send(
            relay.at[way, e], w2g.at[x * 2 + 1 - far, pl.ds(512 * way + 256 * e, 256)],
            zs.at[way, e, 1], zr.at[way, e, 1], z_dev(hop),
        )

    def z_wait(way, e):
        arrive(far_quarter(x, 2 * way + e), zs.at[way, e, 1], zr.at[way, e, 1])

    local[0].wait()
    local[1].wait()
    for j in range(2):
        for way in range(2):
            w1_send(way, 0, j)
    local[2].wait()
    for e in range(2):
        for way in range(2):
            z_first(way, e)
            near_send(way, e)
    for copy in local[3:]:
        copy.wait()

    weight = cnt_v[...].astype(F32)
    wown[...] = jnp.broadcast_to(weight, (8, 128))

    def send_counts():
        for d in range(1, 8):
            send(wown, wrow.at[d - 1], nrs.at[d - 1], nrr.at[d - 1], row_dev(d))
            send(wown, wcol.at[d - 1], ncs.at[d - 1], ncr.at[d - 1], col_dev(d))

    def group(g):
        step, j = (0, 0) if g == 0 else ((g + 1) // 2, (g - 1) % 2)
        first = chunk(0, step, j)
        second = chunk(1, step, j)
        return first, second

    def partial_sum(g):
        (na, ha), (nb, hb) = group(g)
        rhs = jnp.concatenate([w1g[na, ha], w1g[nb, hb]], axis=1)
        acc = jnp.dot(act[...], rhs, preferred_element_type=F32) * SCALE_HIDDEN
        own = []
        for n, half in ((na, ha), (nb, hb)):
            mine = jnp.where(n == t, 1.0, 0.0).astype(F32)
            own.append(res[:, HALF * half : HALF * half + HALF].astype(F32) * mine)
        acc = acc + jnp.concatenate(own, axis=1)
        part[g] = acc.astype(BF).reshape(2, 4, SEL, BLK)

    def stage0(g):
        partial_sum(g)
        send(part.at[g, 1 - core], cin.at[g], crs.at[g], crr.at[g], other)

    def stage1(i):
        arrive(cin.at[i], crs.at[i], crr.at[i])
        both = part[i, core].astype(F32) + cin[i].astype(F32)
        zb[i] = both.astype(BF)
        for d in range(1, 4):
            send(
                zb.at[i, lax.rem(zl + d, 4)], zin.at[i, d - 1],
                zrs.at[i, d - 1], zrr.at[i, d - 1], zl_dev(d),
            )

    def stage2(i):
        total = zb[i, zl].astype(F32)
        for d in range(1, 4):
            arrive(zin.at[i, d - 1], zrs.at[i, d - 1], zrr.at[i, d - 1])
            total = total + zin[i, d - 1].astype(F32)
        y[i, core, zl] = total.astype(BF)
        for d in range(1, 4):
            ref = y.at[i, core, zl]
            send(ref, ref, ags.at[i, d - 1], agr.at[i, d - 1], zl_dev(d))

    def stage3(i):
        for d in range(1, 4):
            arrive(y.at[i, core, lax.rem(zl + 4 - d, 4)], ags.at[i, d - 1], agr.at[i, d - 1])
        ref = y.at[i, core]
        send(ref, ref, cgs.at[i], cgr.at[i], other)

    def stage4(i):
        arrive(y.at[i, 1 - core], cgs.at[i], cgr.at[i])

    def place(d):
        at = lax.rem(t + d, 8)
        return lax.rem(at, 2), lax.div(at, 2)

    def last_out():
        partial_sum(7)
        for d in range(1, 8):
            send(part.at[(7, *place(d))], lin.at[d - 1], lrs.at[d - 1], lrr.at[d - 1], tp_dev(d))

    def last_back():
        total = part[7, core, zl].astype(F32)
        for d in range(1, 8):
            arrive(lin.at[d - 1], lrs.at[d - 1], lrr.at[d - 1])
            total = total + lin[d - 1].astype(F32)
        y[7, core, zl] = total.astype(BF)
        for d in range(1, 8):
            ref = y.at[7, core, zl]
            send(ref, ref, lgs.at[d - 1], lgr.at[d - 1], tp_dev(d))

    def last_wait():
        for d in range(1, 8):
            arrive(y.at[(7, *place(8 - d))], lgs.at[d - 1], lgr.at[d - 1])

    def rows_at(start):
        return (
            lax.broadcasted_iota(jnp.int32, (SEL, BLK), 0) + start
            == lax.broadcasted_iota(jnp.int32, (SEL, BLK), 1)
        ).astype(F32).astype(BF)

    first_rows = rows_at(0)
    other_rows = rows_at(HALF)

    def y_group(g):
        return y[g].reshape(TOK, BLK)

    def back(step):
        return lax.rem(r + 8 - step, 8)

    def ahead(step):
        return lax.rem(r + step, 8)

    def pick_y(n, g, rows):
        sely[n] = lax.dot_general(rows, y_group(g), NT, preferred_element_type=F32).astype(BF)

    def pick_pair(step):
        pick_y(back(step), 2 * step - 1, first_rows)
        pick_y(ahead(step), 2 * step, other_rows)

    def pick_w(n):
        selw[n] = w2g[n][:, :HALF].T[:SEL]

    def product(values, n):
        return lax.dot_general(values, w2g[n], NT, preferred_element_type=F32)

    def pair(step):
        low, high = y_group(2 * step - 1), y_group(2 * step)
        behind = jnp.concatenate([low[:, :HALF], high[:, :HALF]], axis=1)
        before = jnp.concatenate([high[:, HALF:], low[:, HALF:]], axis=1)
        return product(behind, back(step)) + product(before, ahead(step))

    def prepare():
        keep_row = (ids[...] != 0).astype(F32)
        across = lax.broadcasted_iota(jnp.int32, (TOK, TOK), 0)
        along = lax.broadcasted_iota(jnp.int32, (TOK, TOK), 1)
        keep_col = jnp.sum(
            jnp.where(across == along, jnp.broadcast_to(keep_row, (TOK, TOK)), 0.0),
            axis=1, keepdims=True,
        )
        up[...] = (up[...].astype(F32) * keep_col).astype(BF)
        stt[...] = lax.dot_general(rows_at(SEL * t), st[...], NT, preferred_element_type=F32) * keep_row
        pc1[...] = lax.dot_general(first_rows[:, :HALF], w1g[r, 0], NT, preferred_element_type=F32)
        pc2[...] = lax.dot_general(first_rows, w2g[c], NT, preferred_element_type=F32)

    stage0(0)
    prepare()

    ring(1)
    for way in range(2):
        z_second(way, 0)
    for way in range(2):
        near_wait(way, 0)
        near_send(way, 2)
    stage0(1)

    ring(2)
    stage0(2)
    for way in range(2):
        z_second(way, 1)
    stage1(0)
    for way in range(2):
        near_wait(way, 1)

    ring(3)
    stage0(3)
    stage1(1)
    stage1(2)
    for way in range(2):
        near_wait(way, 2)
    for k in range(4):
        pick_w(2 * k + zh)

    ring(4)
    stage0(4)
    stage2(0)
    stage1(3)
    for way in range(2):
        z_wait(way, 0)
    for e in range(2):
        for way in range(2):
            far_send(way, e)
    stage2(1)
    stage1(4)

    ring(5)
    stage0(5)
    stage2(2)
    for way in range(2):
        z_wait(way, 1)
    for e in range(2, 4):
        for way in range(2):
            far_send(way, e)
    stage3(0)
    stage2(3)
    stage1(5)
    stage3(1)
    stage4(0)
    pick_y(r, 0, first_rows)

    ring(6)
    for way in range(2):
        far_wait(way, 0)
        far_send(way, 4)
    stage0(6)
    stage1(6)
    stage2(4)
    stage3(2)
    stage4(1)
    stage2(5)
    stage4(2)
    pick_pair(1)

    ring(7)
    last_out()
    stage2(6)
    for way in range(2):
        far_wait(way, 2)
        far_send(way, 5)
    stage3(3)
    stage3(4)
    stage4(3)
    stage4(4)
    stage3(5)
    last_back()
    stage3(6)
    for way in range(2):
        for e in (1, 3, 4, 5):
            far_wait(way, e)
    for k in range(4):
        pick_w(2 * k + 1 - zh)
    pre2[...] = product(y_group(0), r) + pair(1)
    pre2[...] += pair(2)
    stage4(5)
    stage4(6)
    pre2[...] += pair(3)
    last_wait()

    last = ahead(4)
    y_last = y_group(7)
    carried = jnp.zeros((BLK, TOK), F32)
    for k in range(4):
        cols = slice(256 * k, 256 * k + 256)
        pre = pre2[:, cols] + lax.dot_general(
            y_last, w2g[last, cols], NT, preferred_element_type=F32
        )
        pre = pre * SCALE_MODEL
        squash = jax.nn.sigmoid(pre)
        piece = (up[:, cols].astype(F32) * squash * (1.0 + pre * (1.0 - squash))).astype(BF)
        slope[:, cols] = piece
        carried = carried + lax.dot_general(
            selw[:, :, cols].reshape(BLK, 256), piece, NT, preferred_element_type=F32
        )
    q[...] = (carried * SCALE_MODEL).astype(BF).reshape(8, SEL, TOK)
    for d in range(1, 8):
        send(q.at[lax.rem(t + d, 8)], qin.at[d - 1], qs.at[d - 1], qr.at[d - 1], tp_dev(d))

    pick_pair(2)
    pick_pair(3)
    pick_y(last, 7, first_rows)
    factor = weight * INNER
    grad = jnp.dot(sely[...].reshape(BLK, TOK), slope[...], preferred_element_type=F32) * SCALE_MODEL
    t2[...] = (factor * grad).astype(BF).reshape(4, 2, SEL, HID)
    for d in range(1, 4):
        send(t2.at[lax.rem(x + d, 4)], t2x.at[d - 1], xs.at[d - 1], xr.at[d - 1], x_dev(d))

    total = q[t].astype(F32) + stt[...]
    for d in range(1, 8):
        arrive(qin.at[d - 1], qs.at[d - 1], qr.at[d - 1])
        total = total + qin[d - 1].astype(F32)
    dy[t] = total.astype(BF)
    for d in range(1, 8):
        ref = dy.at[t]
        send(ref, ref, ds_.at[d - 1], dr_.at[d - 1], tp_dev(d))
    send_counts()
    for d in range(1, 8):
        arrive(dy.at[lax.rem(t + 8 - d, 8)], ds_.at[d - 1], dr_.at[d - 1])
    grad = jnp.dot(dy[...].reshape(BLK, TOK), act[...], preferred_element_type=F32) * SCALE_HIDDEN
    t1[...] = (factor * grad).astype(BF).reshape(8, SEL, HID)

    def row_send(d):
        send(t1.at[lax.rem(r + d, 8)], t1in.at[d - 1], rs_.at[d - 1], rr_.at[d - 1], row_dev(d))

    before_rows = len(pending)
    joint = jnp.where(core == 0, 5, 3)
    send(t1.at[lax.rem(r + 4, 8)], t1in.at[3], rs_.at[3], rr_.at[3], row_dev(jnp.where(core == 0, 7, 1)))
    row_send(8 - joint)
    row_send(2)
    row_send(6)

    far = t2[x, 1 - zh].astype(F32)
    near = t2[x, zh].astype(F32)
    for d in range(1, 4):
        arrive(t2x.at[d - 1], xs.at[d - 1], xr.at[d - 1])
        far = far + t2x[d - 1, 1 - zh].astype(F32)
        near = near + t2x[d - 1, zh].astype(F32)
    t2z[...] = far.astype(BF)
    send(t2z, t2zin, as_, ar_, antipode)

    arrive(t1in.at[3], rs_.at[3], rr_.at[3])
    to = lax.rem(r + joint, 8)
    t1[to] = (t1[to].astype(F32) + t1in[3].astype(F32)).astype(BF)
    row_send(joint)
    row_send(1)
    row_send(7)

    def total_of(buffer, s_sems, r_sems):
        count = wown[...]
        for d in range(1, 8):
            arrive(buffer.at[d - 1], s_sems.at[d - 1], r_sems.at[d - 1])
            count = count + buffer[d - 1]
        return count[0:1, 0:1]

    total_one = total_of(wrow, nrs, nrr)
    total_two = total_of(wcol, ncs, ncr)

    arrive(t2zin, as_, ar_)
    delta = (near + t2zin[...].astype(F32)) / total_two
    moment = DECAY * m2[...] + delta
    n2[...] = moment
    o2[...] = pc2[...] - OUTER * (delta + DECAY * moment)

    for copy in pending[:before_rows]:
        copy.wait_send()
    summed = t1[r].astype(F32)
    for d in (2, 6, 3, 5, 1, 7):
        arrive(t1in.at[d - 1], rs_.at[d - 1], rr_.at[d - 1])
        summed = summed + t1in[d - 1].astype(F32)
    delta = summed / total_one
    moment = DECAY * m1[...] + delta
    n1[...] = moment
    o1[...] = pc1[...] - OUTER * (delta + DECAY * moment)

    for copy in pending[before_rows:]:
        copy.wait_send()


def write_out(a, b, c, d, a_out, b_out, c_out, d_out, sems):
    copies = [
        pltpu.make_async_copy(src, dst, sems.at[k])
        for k, (src, dst) in enumerate(((a, a_out), (b, b_out), (c, c_out), (d, d_out)))
    ]
    for copy in copies:
        copy.start()
    for copy in copies:
        copy.wait()


def in_hbm(value):
    return pltpu.with_memory_space_constraint(value, pltpu.HBM)


def on_device(
    act_one, residual, upstream, stream_grad, token_ids, shard_counts,
    out_one, in_two, out_one_moment, in_two_moment,
):
    dma = pltpu.SemaphoreType.DMA
    vmem = pltpu.VMEM
    whole = pl.BlockSpec(memory_space=pltpu.HBM)
    inside = pl.BlockSpec(memory_space=pltpu.VMEM)
    scratch = [
        vmem((TOK, HID), BF), vmem((TOK, BLK), BF), vmem((TOK, HID), BF), vmem((TOK, BLK), BF),
        vmem((1, TOK), jnp.int32), vmem((8, 2, HID, HALF), BF), vmem((8, HID, BLK), BF),
        vmem((SEL, HID), F32), vmem((SEL, HID), F32),
        vmem((8, 2, 4, SEL, BLK), BF), vmem((7, 4, SEL, BLK), BF), vmem((7, SEL, BLK), BF),
        vmem((7, 4, SEL, BLK), BF), vmem((7, 3, SEL, BLK), BF),
        vmem((8, 2, 4, SEL, BLK), BF), vmem((2, 2, BLK, BLK), BF),
        vmem((TOK, HID), F32), vmem((TOK, HID), BF), vmem((8, SEL, HID), BF),
        vmem((8, SEL, TOK), BF), vmem((SEL, TOK), F32), vmem((SEL, HID), F32), vmem((SEL, HID), F32),
        vmem((8, SEL, TOK), BF), vmem((7, SEL, TOK), BF), vmem((8, SEL, TOK), BF),
        vmem((8, SEL, HID), BF), vmem((7, SEL, HID), BF),
        vmem((4, 2, SEL, HID), BF), vmem((3, 2, SEL, HID), BF),
        vmem((SEL, HID), BF), vmem((SEL, HID), BF),
        vmem((8, 128), F32), vmem((7, 8, 128), F32), vmem((7, 8, 128), F32),
        dma((10,)),
        dma((2, 4, 2)), dma((2, 4, 2)), dma((2, 9)), dma((2, 9)), dma((2, 2, 2)), dma((2, 2, 2)),
        dma((7,)), dma((7,)), dma((7, 3)), dma((7, 3)), dma((7, 3)), dma((7, 3)), dma((7,)), dma((7,)),
        dma((7,)), dma((7,)), dma((7,)), dma((7,)),
        dma((7,)), dma((7,)), dma((7,)), dma((7,)), dma((7,)), dma((7,)),
        dma((3,)), dma((3,)), dma(()), dma(()), dma((7,)), dma((7,)), dma((7,)), dma((7,)),
    ]
    result = jax.ShapeDtypeStruct((SEL, HID), F32)
    o1, n1, o2, n2 = pl.pallas_call(
        kernel,
        out_shape=(result,) * 4,
        in_specs=[whole] * 5 + [inside] + [whole] * 4,
        out_specs=(inside,) * 4,
        scratch_shapes=scratch,
        compiler_params=pltpu.CompilerParams(
            collective_id=0, has_side_effects=True, vmem_limit_bytes=48 * 1024 * 1024
        ),
        cost_estimate=pl.CostEstimate(flops=3_000_000_000, bytes_accessed=4_000_000, transcendentals=300_000),
    )(
        *map(in_hbm, (act_one[0, 0], residual[0, 0], upstream[0, 0], stream_grad[0, 0], token_ids[0])),
        shard_counts,
        *map(in_hbm, (out_one[0], in_two[0], out_one_moment[0].T, in_two_moment[0].T)),
    )
    o1, n1, o2, n2 = pl.pallas_call(
        write_out,
        out_shape=(result,) * 4,
        in_specs=[pl.BlockSpec(memory_space=pl.ANY)] * 4,
        out_specs=(whole,) * 4,
        scratch_shapes=[dma((4,))],
        compiler_params=pltpu.CompilerParams(vmem_limit_bytes=1024 * 1024),
    )(o1, n1, o2, n2)
    return (o1.T[None], n1.T[None], o2.T[None], n2.T[None])


def solution(mesh):
    return jax.shard_map(
        on_device,
        mesh=mesh,
        in_specs=(
            P("row", "col", None, "tp"),
            P("row", "col", None, "tp"),
            P("row", "col", None, "tp"),
            P("row", "col", None, None),
            P("row", "col", None),
            P("row", "col"),
            P("col", "tp", "row"),
            P("row", "tp", "col"),
            P("col", "tp", "row"),
            P("row", "tp", "col"),
        ),
        out_specs=(
            P("col", "tp", "row"),
            P("col", "tp", "row"),
            P("row", "tp", "col"),
            P("row", "tp", "col"),
        ),
        check_vma=False,
    )
```
